128 devices in a mesh: leaf: 16 (over z, y), blk: 8 (over x, core).
Axes of the slice: x: 4, y: 4, z: 4, core: 2. Of those that a mesh axis runs over, the one named last changes fastest.
Arguments:
- loads: float32 [3, 16384, 128], P(None, ('leaf', 'blk')), may hold values from -6 to 6
- inverse_root: bfloat16 [16, 8, 2048, 1024], P('leaf', 'blk'), as said below
- inverse_middle: bfloat16 [16, 8, 1024, 1024], P('leaf', 'blk'), as said below
- inverse_lower: bfloat16 [16, 8, 512, 1024], P('leaf', 'blk'), as said below
- couple_middle: bfloat16 [16384, 8192], P(('leaf', 'blk')), may hold values from -0.0625 to 0.0625
- couple_lower: bfloat16 [16384, 4096], P(('leaf', 'blk')), may hold values from -0.09375 to 0.09375
- couple_between: bfloat16 [16384, 4096], P(('leaf', 'blk')), may hold values from -0.09375 to 0.09375
- pattern_middle: int32 [2, 64], replicated, may hold values from 0 to 127, as said below
- pattern_lower: int32 [4, 32], replicated, may hold values from 0 to 127, as said below
- pattern_between: int32 [4, 32], replicated, may hold values from 0 to 63, as said below
- node_blocks: int32 [7], replicated, may hold values from 16 to 128, as said below
Outputs:
- forward: bfloat16 [3, 16384, 128], P(None, ('leaf', 'blk'))
- solution: bfloat16 [3, 16384, 128], P(None, ('leaf', 'blk'))
The draws below stay inside these ranges and needn't reach their ends.
Inputs may be any that keep to these rules, and one draw needn't show every extreme that they name: `inverse_root`: each M_(k,n) is lower triangular, with diagonal entries between 1 and 4. `inverse_middle`: each M_(k,n) is lower triangular, with diagonal entries between 1 and 4. `inverse_lower`: each M_(k,n) is lower triangular, with diagonal entries between 1 and 4. `pattern_middle`: each row holds distinct block numbers of the ancestor node, among them its first and its last block. `pattern_lower`: each row holds distinct block numbers of the ancestor node, among them its first and its last block. `pattern_between`: each row holds distinct block numbers of the ancestor node, among them its first and its last block. `node_blocks`: entry 2**k - 1 + n counts the live blocks of node n of level k: between half and all of its (16 >> k) * 8 blocks. The root's blocks are all live; on levels 1 and 2 some node has all its blocks live and some node exactly half.
All inputs are finite; a program needn't handle non-finite values.
Results may differ from the reference program's by a relative error of at most 0.029.
Values may be sent and summed in bfloat16 or wider, within the bound.
No kernel may reach another device: no remote copies, remote signals or barrier semaphores. Data moves between devices by JAX's collectives and lax.ppermute only.
A program may use at most 128 MiB of HBM per device.

```python
import math
import jax
import jax.numpy as jnp
from jax import lax

BLOCK = 128
LOADS = 128
LEVELS = 3
ROWS = 16384
N_LEAF = 16
N_BLK = 8


def inverse_shape(tree_level):
    return (N_LEAF, N_BLK, (N_LEAF >> tree_level) * BLOCK, N_BLK * BLOCK)


def triangle(raw_values, tree_level):
    group_size = N_LEAF >> tree_level
    span = group_size * N_BLK * BLOCK
    leaf_position = lax.broadcasted_iota(jnp.int32, (N_LEAF, 1, 1, 1), 0) % group_size
    blk_position = lax.broadcasted_iota(jnp.int32, (1, N_BLK, 1, 1), 1)
    row_position = lax.broadcasted_iota(jnp.int32, (1, 1, group_size * BLOCK, 1), 2)
    column_position = lax.broadcasted_iota(jnp.int32, (1, 1, 1, N_BLK * BLOCK), 3)
    row_index = (row_position // BLOCK * N_BLK + blk_position) * BLOCK + row_position % BLOCK
    column_index = (leaf_position * N_BLK + column_position // BLOCK) * BLOCK + column_position % BLOCK
    below_part = raw_values * (0.7 / math.sqrt(span))
    diagonal = 1.0 + 0.5 * jnp.abs(raw_values)
    filled = jnp.where(row_index > column_index, below_part, jnp.where(row_index == column_index, diagonal, 0.0))
    return filled.astype(jnp.bfloat16)


def draw_inverse_root(key, part):
    key = jax.random.fold_in(key, 3)
    raw_values = jax.random.normal(key, inverse_shape(0), jnp.float32)
    return triangle(raw_values, 0)


def draw_inverse_middle(key, part):
    key = jax.random.fold_in(key, 5)
    raw_values = jax.random.normal(key, inverse_shape(1), jnp.float32)
    return triangle(raw_values, 1)


def draw_inverse_lower(key, part):
    key = jax.random.fold_in(key, 7)
    raw_values = jax.random.normal(key, inverse_shape(2), jnp.float32)
    return triangle(raw_values, 2)


def pattern_rows(key, lower_level, upper_level):
    node_count = 2 ** lower_level
    chosen_count = (N_LEAF >> lower_level) * N_BLK
    available = (N_LEAF >> upper_level) * N_BLK

    def one_node(node_key):
        inner = jax.random.permutation(node_key, available - 2)[:chosen_count - 2].astype(jnp.int32) + 1
        first = jnp.zeros((1,), jnp.int32)
        final = jnp.full((1,), available - 1, jnp.int32)
        return jnp.concatenate([first, inner, final])
    return jax.vmap(one_node)(jax.random.split(key, node_count))


def draw_pattern_middle(key, part):
    key = jax.random.fold_in(key, 11)
    return pattern_rows(key, 1, 0)


def draw_pattern_lower(key, part):
    key = jax.random.fold_in(key, 13)
    return pattern_rows(key, 2, 0)


def draw_pattern_between(key, part):
    key = jax.random.fold_in(key, 17)
    return pattern_rows(key, 2, 1)


def draw_node_blocks(key, part):
    key = jax.random.fold_in(key, 19)
    pieces = [jnp.full((1,), N_LEAF * N_BLK, jnp.int32)]
    for tree_level in (1, 2):
        capacity = (N_LEAF >> tree_level) * N_BLK
        node_count = 2 ** tree_level
        key, value_key, order_key = jax.random.split(key, 3)
        values = jax.random.randint(value_key, (node_count,), capacity // 2, capacity + 1, dtype=jnp.int32)
        ordering = jax.random.permutation(order_key, node_count)
        values = values.at[ordering[0]].set(capacity).at[ordering[1]].set(capacity // 2)
        pieces.append(values)
    return jnp.concatenate(pieces)


def levels(stream_key, shape, cuts, low, high):
    factor_of = 1.0
    for dim, shards_of in cuts:
        heights = jax.random.uniform(jax.random.fold_in(jax.random.fold_in(stream_key, 6), dim), (shards_of,), jnp.float32, low / len(cuts), high / len(cuts))
        factor_of = factor_of * jnp.repeat(jnp.exp(heights), shape[dim] // shards_of).reshape((-1,) + (1,) * (len(shape) - 1 - dim))
    return factor_of


def normal_values(own_key, extent, spread, bound, cuts=(), kind=jnp.bfloat16):
    entries = spread * jax.random.normal(own_key, extent, jnp.float32)
    if cuts:
        entries = entries * levels(own_key, extent, cuts, -0.22, 0.18)
    return jnp.clip(entries, -bound, bound).astype(kind)


def setup_inputs(seed: int = 0) -> dict:
    splits = jax.random.split(jax.random.key(seed), 12)
    return {
        "loads": normal_values(splits[0], (LEVELS, ROWS, LOADS), 1.0, 6.0, ((1, 128),), jnp.float32),
        "inverse_root": draw_inverse_root(jax.random.fold_in(splits[11], 71), 0),
        "inverse_middle": draw_inverse_middle(jax.random.fold_in(splits[11], 71), 0),
        "inverse_lower": draw_inverse_lower(jax.random.fold_in(splits[11], 71), 0),
        "couple_middle": normal_values(splits[4], (ROWS, N_LEAF // 2 * N_BLK * BLOCK), (N_LEAF // 2 * N_BLK * BLOCK) ** -0.5, 0.0625, ((0, 128),)),
        "couple_lower": normal_values(splits[5], (ROWS, N_LEAF // 4 * N_BLK * BLOCK), (N_LEAF // 4 * N_BLK * BLOCK) ** -0.5, 0.09375, ((0, 128),)),
        "couple_between": normal_values(splits[6], (ROWS, N_LEAF // 4 * N_BLK * BLOCK), (N_LEAF // 4 * N_BLK * BLOCK) ** -0.5, 0.09375, ((0, 128),)),
        "pattern_middle": draw_pattern_middle(jax.random.fold_in(splits[11], 71), 0),
        "pattern_lower": draw_pattern_lower(jax.random.fold_in(splits[11], 71), 0),
        "pattern_between": draw_pattern_between(jax.random.fold_in(splits[11], 71), 0),
        "node_blocks": draw_node_blocks(jax.random.fold_in(splits[11], 71), 0),
    }


def level_span(tree_level):
    return (N_LEAF >> tree_level) * N_BLK * BLOCK


def apply_inverse(inverse_tiles, vector, tree_level, transposed):
    group_size = N_LEAF >> tree_level
    node_count = 2 ** tree_level
    load_count = vector.shape[-1]
    blocks = vector.astype(jnp.float32).reshape(node_count, group_size, N_BLK, BLOCK, load_count)

    def visit(position, accumulated):
        node_index = position // group_size
        leaf_index = position % group_size
        inverse_tile = inverse_tiles[position].astype(jnp.float32).reshape(N_BLK, group_size, BLOCK, N_BLK, BLOCK)
        if transposed:
            contribution = jnp.einsum("jmrkc,mjrx->kcx", inverse_tile, blocks[node_index])
            return accumulated.at[node_index, leaf_index].add(contribution)
        contribution = jnp.einsum("jmrkc,kcx->mjrx", inverse_tile, blocks[node_index, leaf_index])
        return accumulated.at[node_index].add(contribution)

    initial = jnp.zeros((node_count, group_size, N_BLK, BLOCK, load_count), jnp.float32)
    return lax.fori_loop(0, N_LEAF, visit, initial).reshape(ROWS, load_count)


def structure_targets(pattern, lower_level, upper_level):
    ancestor = jnp.arange(2 ** lower_level, dtype=jnp.int32) // (2 ** (lower_level - upper_level))
    return (ancestor[:, None] * (level_span(upper_level) // BLOCK) + pattern).reshape(-1)


def lift_updates(coupling, pattern, solved, lower_level, upper_level):
    span = level_span(lower_level)
    node_count = 2 ** lower_level
    load_count = solved.shape[-1]
    factor = coupling.astype(jnp.float32).reshape(node_count, span, span)
    values = solved.astype(jnp.float32).reshape(node_count, span, load_count)
    updates = jnp.einsum("spt,spx->stx", factor, values).reshape(-1, BLOCK, load_count)
    targets = structure_targets(pattern, lower_level, upper_level)
    placed = jnp.zeros((ROWS // BLOCK, BLOCK, load_count), jnp.float32).at[targets].add(updates)
    return placed.reshape(ROWS, load_count)


def pull_values(coupling, pattern, upper_solution, lower_level, upper_level):
    span = level_span(lower_level)
    node_count = 2 ** lower_level
    load_count = upper_solution.shape[-1]
    factor = coupling.astype(jnp.float32).reshape(node_count, span, span)
    blocks = upper_solution.astype(jnp.float32).reshape(ROWS // BLOCK, BLOCK, load_count)
    chosen = blocks[structure_targets(pattern, lower_level, upper_level)].reshape(node_count, span, load_count)
    return jnp.einsum("spt,stx->spx", factor, chosen).reshape(ROWS, load_count)


def live_mask(node_blocks, tree_level):
    capacity = level_span(tree_level) // BLOCK
    block_number = jnp.arange(ROWS, dtype=jnp.int32) // BLOCK
    limit = node_blocks[2 ** tree_level - 1 + block_number // capacity]
    return ((block_number % capacity) < limit).astype(jnp.float32)[:, None]


def solve_lower(inverse_tiles, residual, node_blocks, tree_level):
    product = apply_inverse(inverse_tiles, residual, tree_level, False)
    return (live_mask(node_blocks, tree_level) * product).astype(jnp.bfloat16)


def solve_upper(inverse_tiles, residual, node_blocks, tree_level):
    product = apply_inverse(inverse_tiles, residual, tree_level, True)
    return (live_mask(node_blocks, tree_level) * product).astype(jnp.bfloat16)


def reference(loads, inverse_root, inverse_middle, inverse_lower, couple_middle, couple_lower, couple_between, pattern_middle, pattern_lower, pattern_between, node_blocks):
    lower_solved = solve_lower(inverse_lower, loads[2].astype(jnp.bfloat16), node_blocks, 2)
    middle_updates = lift_updates(couple_between, pattern_between, lower_solved, 2, 1)
    middle_residual = (loads[1] - middle_updates).astype(jnp.bfloat16)
    middle_solved = solve_lower(inverse_middle, middle_residual, node_blocks, 1)
    root_updates = lift_updates(couple_middle, pattern_middle, middle_solved, 1, 0) + lift_updates(couple_lower, pattern_lower, lower_solved, 2, 0)
    root_residual = (loads[0] - root_updates).astype(jnp.bfloat16)
    root_solved = solve_lower(inverse_root, root_residual, node_blocks, 0)
    root_answer = solve_upper(inverse_root, root_solved, node_blocks, 0)
    middle_pull = pull_values(couple_middle, pattern_middle, root_answer, 1, 0)
    middle_reduced = (middle_solved.astype(jnp.float32) - middle_pull).astype(jnp.bfloat16)
    middle_answer = solve_upper(inverse_middle, middle_reduced, node_blocks, 1)
    lower_pull = pull_values(couple_lower, pattern_lower, root_answer, 2, 0) + pull_values(couple_between, pattern_between, middle_answer, 2, 1)
    lower_reduced = (lower_solved.astype(jnp.float32) - lower_pull).astype(jnp.bfloat16)
    lower_answer = solve_upper(inverse_lower, lower_reduced, node_blocks, 2)
    forward = jnp.stack([root_solved, middle_solved, lower_solved])
    solution = jnp.stack([root_answer, middle_answer, lower_answer])
    return (forward, solution)
```

```python
import functools

import jax
import jax.numpy as jnp
from jax import lax
from jax.experimental import pallas as pl
from jax.experimental.pallas import tpu as pltpu
from jax.sharding import PartitionSpec as P

BF16 = jnp.bfloat16
F32 = jnp.float32
VMEM_LIMIT = 48 * 1024 * 1024


def lift_kernel(level_spans, info, *refs):
    total = len(level_spans)
    patterns, values, factors = refs[:total], refs[total : 2 * total], refs[2 * total : 3 * total]
    keep, send, sums = refs[3 * total :]
    core = info[0]
    sums[...] = jnp.zeros_like(sums)
    half = keep.shape[0]
    for index, span in enumerate(level_spans):
        node = info[1 + index]
        value = values[index][...]

        def chunk(step, carry, index=index, node=node, value=value):
            start = pl.multiple_of(step * 1024, 1024)
            product = jnp.dot(
                value, factors[index][:, pl.ds(start, 1024)], preferred_element_type=F32
            )
            for part in range(8):
                block = patterns[index][node, step * 8 + part]
                slot = ((block & 1) ^ core) * half + (block >> 1)
                sums[slot] += product[:, part * 128 : part * 128 + 128]
            return carry

        lax.fori_loop(0, span // 1024, chunk, 0)

    def emit(slot, carry):
        keep[slot] = sums[slot].astype(BF16)
        send[slot] = sums[half + slot].astype(BF16)
        return carry

    lax.fori_loop(0, half, emit, 0)


def lift(info, patterns, values, factors, half):
    spans = tuple(f.shape[1] for f in factors)
    smem = pl.BlockSpec(memory_space=pltpu.SMEM)
    vmem = pl.BlockSpec(memory_space=pltpu.VMEM)
    total = len(factors)
    shape = jax.ShapeDtypeStruct((half, 128, 128), BF16)
    return pl.pallas_call(
        functools.partial(lift_kernel, spans),
        out_shape=(shape, shape),
        in_specs=[smem] * (1 + total) + [vmem] * (2 * total),
        out_specs=(vmem, vmem),
        scratch_shapes=[pltpu.VMEM((2 * half, 128, 128), F32)],
        compiler_params=pltpu.CompilerParams(vmem_limit_bytes=VMEM_LIMIT),
        name="lift",
    )(info, *patterns, *values, *factors)


def pull_kernel(info, pattern, own, other, factor, out, chosen):
    core, node = info[0], info[1]
    count = factor.shape[1] // 128

    def pick(position, carry):
        block = pattern[node, position]
        mine = (block & 1) == core
        row = pl.multiple_of(position * 128, 128)
        chosen[pl.ds(row, 128), :] = jnp.where(mine, own[block >> 1], other[block >> 1])
        return carry

    lax.fori_loop(0, count, pick, 0)
    out[...] = jnp.dot(factor[...], chosen[...], preferred_element_type=F32)


def pull(info, pattern, own, other, factor):
    smem = pl.BlockSpec(memory_space=pltpu.SMEM)
    vmem = pl.BlockSpec(memory_space=pltpu.VMEM)
    return pl.pallas_call(
        pull_kernel,
        out_shape=jax.ShapeDtypeStruct((128, 128), F32),
        in_specs=[smem, smem, vmem, vmem, vmem],
        out_specs=vmem,
        scratch_shapes=[pltpu.VMEM((factor.shape[1], 128), BF16)],
        compiler_params=pltpu.CompilerParams(vmem_limit_bytes=VMEM_LIMIT),
        name="pull",
    )(info, pattern, own, other, factor)


def shards(
    loads,
    inverse_root,
    inverse_middle,
    inverse_lower,
    couple_middle,
    couple_lower,
    couple_between,
    pattern_middle,
    pattern_lower,
    pattern_between,
    node_blocks,
):
    leaf_count = lax.axis_size("leaf")
    block_count = lax.axis_size("blk")
    chip_count = block_count // 2
    leaf_index = lax.axis_index("leaf")
    block_index = lax.axis_index("blk")
    core = block_index & 1
    chip = block_index >> 1
    leaf_bits = leaf_count.bit_length() - 1

    def node_of(level):
        return leaf_index >> (leaf_bits - level)

    def leaf_groups(level):
        size = leaf_count >> level
        return [[g * size + j for j in range(size)] for g in range(1 << level)]

    chip_groups = [[2 * x + c for x in range(chip_count)] for c in range(2)]

    def limit_of(level):
        return node_blocks[2**level - 1 + node_of(level)]

    def live_own(level):
        position = (leaf_index & ((leaf_count >> level) - 1)) * block_count + block_index
        return (position < limit_of(level)).astype(F32)

    def live_chips(level):
        position = (leaf_index & ((leaf_count >> level) - 1)) * block_count + core
        position = position + 2 * jnp.arange(chip_count)
        return (position < limit_of(level)).astype(F32)[:, None, None]

    def swap_core(value):
        return lax.ppermute(value, "blk", [(i, i ^ 1) for i in range(block_count)])

    def swap_chip(value, first):
        pairs = []
        for i in range(block_count):
            near = (i & 1 == 0) == first
            pairs.append((i, i ^ (2 if near else 6)))
        return lax.ppermute(value, "blk", pairs)

    def exchange(value, level):
        groups = leaf_groups(level) if level else None
        return lax.all_to_all(value, "leaf", 0, 0, tiled=True, axis_index_groups=groups)

    def reduce_leaf(partial_value, level):
        return exchange(partial_value.astype(BF16), level).astype(F32).sum(0)

    def gather_leaf(value, level):
        size = leaf_count >> level
        return exchange(jnp.broadcast_to(value[None], (size,) + value.shape), level)

    def sum_chips(value):
        value = value + swap_chip(value.astype(BF16), True).astype(F32)
        return value + swap_chip(value.astype(BF16), False).astype(F32)

    def both_cores(value):
        other = swap_core(value)
        return jnp.where(
            core == 0, jnp.stack([value, other], 1), jnp.stack([other, value], 1)
        )

    def sum_cores(partial_value):
        mine = jnp.where(core == 0, partial_value[:, 0], partial_value[:, 1])
        theirs = jnp.where(core == 0, partial_value[:, 1], partial_value[:, 0])
        return mine + swap_core(theirs.astype(BF16)).astype(F32)

    def own_chip(blocks):
        return lax.dynamic_index_in_dim(blocks, chip, 0, keepdims=False)

    chip_mask = (jnp.arange(chip_count) == chip).astype(F32)[:, None, None]

    def info_of(*levels):
        return jnp.stack([core.astype(jnp.int32)] + [node_of(k).astype(jnp.int32) for k in levels])

    def residual(load, updates, level):
        keep, send = updates
        size = leaf_count >> level
        summed = (keep.astype(F32) + swap_core(send).astype(F32)).astype(BF16)
        partial_sum = reduce_leaf(summed.reshape(size, chip_count, 128, 128), level)
        partial_rest = chip_mask * load.T[None] - partial_sum
        rest = both_cores(sum_chips(partial_rest).astype(BF16))
        return rest.reshape(block_count, 128, 128)

    def forward_solve(tile, rest, level, transposed):
        size = leaf_count >> level
        columns = rest.swapaxes(1, 2) if transposed else rest
        partial_value = jnp.dot(
            tile[0, 0], columns.reshape(-1, 128), preferred_element_type=F32
        )
        return reduce_leaf(partial_value.reshape(size, 128, 128), level)

    def backward_partial(tile, value, level):
        gathered = gather_leaf(value, level).reshape(-1, 128)
        partial_value = lax.dot_general(
            tile[0, 0], gathered, (((0,), (0,)), ((), ())), preferred_element_type=F32
        )
        return sum_cores(partial_value.reshape(chip_count, 2, 128, 128))

    load_lower = loads[2].astype(BF16)
    near = lax.all_to_all(
        jnp.broadcast_to(load_lower[None], (chip_count, 128, 128)),
        "blk", 0, 0, tiled=True, axis_index_groups=chip_groups,
    )
    rest_lower = both_cores(near).reshape(block_count, 128, 128)
    y_lower = (forward_solve(inverse_lower, rest_lower, 2, False) * live_own(2)).astype(BF16)
    updates = lift(
        info_of(2), [pattern_between], [y_lower.T], [couple_between],
        (leaf_count >> 1) * chip_count,
    )
    rest_middle = residual(loads[1], updates, 1)
    y_middle = (forward_solve(inverse_middle, rest_middle, 1, True) * live_own(1)).astype(BF16)
    updates = lift(
        info_of(2, 1), [pattern_lower, pattern_middle], [y_lower.T, y_middle.T],
        [couple_lower, couple_middle], leaf_count * chip_count,
    )
    rest_root = residual(loads[0], updates, 0)
    y_root = (forward_solve(inverse_root, rest_root, 0, True) * live_own(0)).astype(BF16)
    x_root = sum_chips(backward_partial(inverse_root, y_root, 0))
    x_root = (x_root * live_chips(0)).astype(BF16)
    own_root = gather_leaf(x_root, 0).reshape(-1, 128, 128)
    other_root = swap_core(own_root)
    pull_middle = pull(info_of(1), pattern_middle, own_root, other_root, couple_middle)
    z_middle = (y_middle.astype(F32) - pull_middle).astype(BF16)
    x_middle = sum_chips(backward_partial(inverse_middle, z_middle, 1))
    x_middle = (x_middle * live_chips(1)).astype(BF16)
    own_middle = gather_leaf(x_middle, 1).reshape(-1, 128, 128)
    other_middle = swap_core(own_middle)
    pull_lower = pull(info_of(2), pattern_lower, own_root, other_root, couple_lower)
    pull_between = pull(info_of(2), pattern_between, own_middle, other_middle, couple_between)
    z_lower = (y_lower.astype(F32) - (pull_lower + pull_between)).astype(BF16)
    x_lower = backward_partial(inverse_lower, z_lower, 2)
    x_lower = lax.all_to_all(
        x_lower.astype(BF16), "blk", 0, 0, tiled=True, axis_index_groups=chip_groups
    )
    x_lower = (x_lower.astype(F32).sum(0) * live_own(2)).astype(BF16)

    forward = jnp.stack([y_root, y_middle, y_lower])
    answer = jnp.stack([own_chip(x_root), own_chip(x_middle), x_lower])
    return (forward, answer)


def solution(mesh):
    in_specs = (
        P(None, ("leaf", "blk"), None),
        P("leaf", "blk", None, None),
        P("leaf", "blk", None, None),
        P("leaf", "blk", None, None),
        P(("leaf", "blk"), None),
        P(("leaf", "blk"), None),
        P(("leaf", "blk"), None),
        P(),
        P(),
        P(),
        P(),
    )
    out_specs = (P(None, ("leaf", "blk"), None), P(None, ("leaf", "blk"), None))
    return jax.shard_map(shards, mesh=mesh, in_specs=in_specs, out_specs=out_specs, check_vma=False)
```

```python
import functools

import jax
import jax.numpy as jnp
from jax import lax
from jax.experimental import pallas as pl
from jax.experimental.pallas import tpu as pltpu
from jax.sharding import PartitionSpec as P

BF16 = jnp.bfloat16
F32 = jnp.float32
MIB = 1024 * 1024
SMEM = pl.BlockSpec(memory_space=pltpu.SMEM)
VMEM = pl.BlockSpec(memory_space=pltpu.VMEM)
CORE, NODE_MIDDLE, NODE_LOWER, LIVE_MIDDLE, LIVE_LOWER = range(5)


def call(kernel, name, out_shape, smem, vmem, scratch=(), limit=24):
    return pl.pallas_call(
        kernel,
        out_shape=out_shape,
        in_specs=[SMEM] * len(smem) + [VMEM] * len(vmem),
        out_specs=jax.tree.map(lambda _: VMEM, out_shape),
        scratch_shapes=list(scratch),
        compiler_params=pltpu.CompilerParams(vmem_limit_bytes=limit * MIB),
        name=name,
    )(*smem, *vmem)


def blocks(count, dtype=BF16):
    return jax.ShapeDtypeStruct((count, 128, 128), dtype)


BLOCK = jax.ShapeDtypeStruct((128, 128), BF16)


def total_of(parts):
    total = parts[0].astype(F32)
    for index in range(1, parts.shape[0]):
        total = total + parts[index].astype(F32)
    return total


def multiply_kernel(transposed, info, own, other, tile, out, columns):
    first = info[CORE] == 0
    for chip in range(own.shape[0]):
        mine, theirs = own[chip], other[chip]
        for core in range(2):
            block = jnp.where(first == (core == 0), mine, theirs)
            row = (2 * chip + core) * 128
            columns[row : row + 128, :] = block.T if transposed else block
    for group in range(out.shape[0]):
        rows = tile[group * 128 : group * 128 + 128, :]
        out[group] = jnp.dot(rows, columns[...], preferred_element_type=F32).astype(BF16)


def multiply(info, own, other, tile, transposed):
    count = tile.shape[0] // 128
    return call(
        functools.partial(multiply_kernel, transposed),
        "multiply",
        blocks(count),
        [info],
        [own, other, tile],
        [pltpu.VMEM((tile.shape[1], 128), BF16)],
    )


def transposed_kernel(info, gathered, tile, mine, theirs):
    first = info[CORE] == 0
    rows = jnp.concatenate([gathered[a] for a in range(gathered.shape[0])], axis=1)
    for chip in range(mine.shape[0]):
        column = chip * 256
        product = jnp.dot(rows, tile[:, column : column + 256], preferred_element_type=F32)
        even, odd = product[:, :128].T, product[:, 128:].T
        mine[chip] = jnp.where(first, even, odd)
        theirs[chip] = jnp.where(first, odd, even).astype(BF16)


def multiply_transposed(info, gathered, tile):
    chips = tile.shape[1] // 256
    return call(
        transposed_kernel,
        "multiply_transposed",
        (blocks(chips, F32), blocks(chips)),
        [info],
        [gathered, tile],
    )


def lift_kernel(spans, nodes, live, info, *refs):
    total = len(spans)
    patterns, refs = refs[:total], refs[total:]
    parts, refs = refs[0], refs[1:]
    earlier, refs = refs[: total - 1], refs[total - 1 :]
    factors, (solved, keep, send, sums) = refs[:total], refs[total:]
    core = info[CORE]
    half = keep.shape[0]
    value = (total_of(parts) * info[live].astype(F32)).astype(BF16)
    solved[...] = value
    values = [value.T] + [e[...].T for e in earlier]
    sums[...] = jnp.zeros_like(sums)
    for index, span in enumerate(spans):
        node = info[nodes[index]]

        def chunk(step, carry, index=index, node=node):
            start = pl.multiple_of(step * 1024, 1024)
            product = jnp.dot(
                values[index], factors[index][:, pl.ds(start, 1024)], preferred_element_type=F32
            )
            for part in range(8):
                block = patterns[index][node, step * 8 + part]
                slot = ((block & 1) ^ core) * half + (block >> 1)
                sums[slot] += product[:, part * 128 : part * 128 + 128]
            return carry

        lax.fori_loop(0, span // 1024, chunk, 0)

    def emit(slot, carry):
        keep[slot] = sums[slot].astype(BF16)
        send[slot] = sums[half + slot].astype(BF16)
        return carry

    lax.fori_loop(0, half, emit, 0)


def lift(info, live, nodes, patterns, parts, earlier, factors, half):
    spans = tuple(f.shape[1] for f in factors)
    return call(
        functools.partial(lift_kernel, spans, nodes, live),
        "lift",
        (BLOCK, blocks(half), blocks(half)),
        [info, *patterns],
        [parts, *earlier, *factors],
        [pltpu.VMEM((2 * half, 128, 128), F32)],
    )


def root_kernel(parts, middle, lower, forward, copies):
    value = total_of(parts).astype(BF16)
    forward[0] = value
    forward[1] = middle[...]
    forward[2] = lower[...]
    turned = value.T
    for index in range(copies.shape[0]):
        copies[index] = turned


def pick_blocks(info, node, pattern, own, other, chosen):
    core, row_of = info[CORE], info[node]

    def pick(position, carry):
        block = pattern[row_of, position]
        mine = (block & 1) == core
        row = pl.multiple_of(position * 128, 128)
        chosen[pl.ds(row, 128), :] = jnp.where(mine, own[block >> 1], other[block >> 1])
        return carry

    lax.fori_loop(0, pattern.shape[1], pick, 0, unroll=4)


def pull_kernel(node, info, pattern, own, other, factor, out, chosen):
    pick_blocks(info, node, pattern, own, other, chosen)
    out[...] = jnp.dot(factor[...], chosen[...], preferred_element_type=F32)


def reduce_kernel(node, earlier, info, pattern, own, other, factor, solved, *refs):
    copies, chosen = refs[-2:]
    pick_blocks(info, node, pattern, own, other, chosen)
    pulled = jnp.dot(factor[...], chosen[...], preferred_element_type=F32)
    if earlier:
        pulled = pulled + refs[0][...]
    turned = (solved[...].astype(F32) - pulled).astype(BF16).T
    for index in range(copies.shape[0]):
        copies[index] = turned


def pull(info, node, pattern, own, other, factor):
    return call(
        functools.partial(pull_kernel, node),
        "pull",
        jax.ShapeDtypeStruct((128, 128), F32),
        [info, pattern],
        [own, other, factor],
        [pltpu.VMEM((factor.shape[1], 128), BF16)],
    )


def reduced(info, node, pattern, own, other, factor, solved, earlier, count):
    return call(
        functools.partial(reduce_kernel, node, bool(earlier)),
        "reduced",
        blocks(count),
        [info, pattern],
        [own, other, factor, solved, *earlier],
        [pltpu.VMEM((factor.shape[1], 128), BF16)],
    )


def last_kernel(info, parts, root, middle, out):
    out[0] = root[...]
    out[1] = middle[...]
    out[2] = (total_of(parts) * info[LIVE_LOWER].astype(F32)).astype(BF16)


def shards(
    loads,
    inverse_root,
    inverse_middle,
    inverse_lower,
    couple_middle,
    couple_lower,
    couple_between,
    pattern_middle,
    pattern_lower,
    pattern_between,
    node_blocks,
):
    leaf_count = lax.axis_size("leaf")
    block_count = lax.axis_size("blk")
    chip_count = block_count // 2
    leaf_index = lax.axis_index("leaf")
    block_index = lax.axis_index("blk")
    core = block_index & 1
    chip = block_index >> 1
    leaf_bits = leaf_count.bit_length() - 1

    def node_of(level):
        return leaf_index >> (leaf_bits - level)

    def leaf_groups(level):
        size = leaf_count >> level
        return [[g * size + j for j in range(size)] for g in range(1 << level)]

    chip_groups = [[2 * x + c for x in range(chip_count)] for c in range(2)]

    def live(level, lane):
        position = (leaf_index & ((leaf_count >> level) - 1)) * block_count + lane
        return position < node_blocks[2**level - 1 + node_of(level)]

    def swap_core(value):
        return lax.ppermute(value, "blk", [(i, i ^ 1) for i in range(block_count)])

    def swap_chip(value, first):
        pairs = []
        for i in range(block_count):
            near = (i & 1 == 0) == first
            pairs.append((i, i ^ (2 if near else 6)))
        return lax.ppermute(value, "blk", pairs)

    info = jnp.stack(
        [core, node_of(1), node_of(2), live(1, block_index), live(2, block_index)]
    ).astype(jnp.int32)
    chip_mask = (jnp.arange(chip_count) == chip).astype(F32)[:, None, None]
    live_middle = live(1, 2 * jnp.arange(chip_count) + core).astype(F32)[:, None, None]
    kept = {
        "info": info,
        "chip_mask": chip_mask,
        "live_middle": live_middle,
        "load_middle": loads[1].T,
        "load_root": loads[0].T,
    }

    def fence(value):
        tied, held = lax.optimization_barrier((value, dict(kept)))
        kept.update(held)
        return tied

    def exchange(value, axis, groups):
        value = fence(value)
        value = lax.all_to_all(value, axis, 0, 0, tiled=True, axis_index_groups=groups)
        return fence(value)

    def over_leaf(value, level):
        return exchange(value, "leaf", leaf_groups(level) if level else None)

    def sum_chips(value):
        for first in (True, False):
            value = (value.astype(F32) + swap_chip(value, first).astype(F32)).astype(BF16)
        return value

    def residual(load, level):
        size = leaf_count >> level
        keep, send = kept.pop("keep"), kept.pop("send")
        summed = (keep.astype(F32) + swap_core(send).astype(F32)).astype(BF16)
        partial_sum = over_leaf(summed.reshape(size, chip_count, 128, 128), level)
        partial_sum = partial_sum.astype(F32).sum(0)
        rest = sum_chips((kept["chip_mask"] * kept[load][None] - partial_sum).astype(BF16))
        return rest, swap_core(rest)

    def backward(gathered, tile):
        mine, theirs = multiply_transposed(kept["info"], gathered, tile)
        return (mine + swap_core(theirs).astype(F32)).astype(BF16)

    def own_chip(value):
        return lax.dynamic_index_in_dim(value, chip, 0, keepdims=False)

    tile_root, tile_middle, tile_lower = inverse_root[0, 0], inverse_middle[0, 0], inverse_lower[0, 0]

    load_lower = loads[2].astype(BF16)
    own = exchange(
        jnp.broadcast_to(load_lower[None], (chip_count, 128, 128)), "blk", chip_groups
    )
    parts = over_leaf(multiply(kept["info"], own, swap_core(own), tile_lower, False), 2)
    y_lower, kept["keep"], kept["send"] = lift(
        kept["info"], LIVE_LOWER, (NODE_LOWER,), [pattern_between], parts, [],
        [couple_between], (leaf_count >> 1) * chip_count,
    )
    kept["y_lower"] = y_lower
    own, other = residual("load_middle", 1)
    parts = over_leaf(multiply(kept["info"], own, other, tile_middle, True), 1)
    y_middle, kept["keep"], kept["send"] = lift(
        kept["info"], LIVE_MIDDLE, (NODE_MIDDLE, NODE_LOWER), [pattern_middle, pattern_lower],
        parts, [kept["y_lower"]], [couple_middle, couple_lower], leaf_count * chip_count,
    )
    kept["y_middle"] = y_middle
    own, other = residual("load_root", 0)
    parts = over_leaf(multiply(kept["info"], own, other, tile_root, True), 0)
    forward, copies = call(
        root_kernel, "root", (blocks(3), blocks(leaf_count)), [],
        [parts, kept["y_middle"], kept["y_lower"]],
    )
    kept["forward"] = forward
    x_root = sum_chips(backward(over_leaf(copies, 0), tile_root))
    kept["x_root"] = own_chip(x_root)
    own = over_leaf(jnp.broadcast_to(x_root[None], (leaf_count,) + x_root.shape), 0)
    own = own.reshape(-1, 128, 128)
    other = swap_core(own)
    copies = reduced(
        kept["info"], NODE_MIDDLE, pattern_middle, own, other, couple_middle,
        kept["y_middle"], [], leaf_count >> 1,
    )
    kept["own_root"], kept["other_root"] = own, other
    x_middle = sum_chips(backward(over_leaf(copies, 1), tile_middle))
    x_middle = (x_middle * kept["live_middle"]).astype(BF16)
    kept["x_middle"] = own_chip(x_middle)
    own = over_leaf(jnp.broadcast_to(x_middle[None], (leaf_count >> 1,) + x_middle.shape), 1)
    own = own.reshape(-1, 128, 128)
    other = swap_core(own)
    pulled = pull(
        kept["info"], NODE_LOWER, pattern_lower, kept.pop("own_root"), kept.pop("other_root"),
        couple_lower,
    )
    copies = reduced(
        kept["info"], NODE_LOWER, pattern_between, own, other, couple_between,
        kept["y_lower"], [pulled], leaf_count >> 2,
    )
    x_lower = backward(over_leaf(copies, 2), tile_lower)
    parts = exchange(x_lower, "blk", chip_groups)
    answer = call(
        last_kernel, "last", blocks(3), [kept["info"]],
        [parts, kept["x_root"], kept["x_middle"]],
    )
    return (kept["forward"], answer)


def solution(mesh):
    in_specs = (
        P(None, ("leaf", "blk"), None),
        P("leaf", "blk", None, None),
        P("leaf", "blk", None, None),
        P("leaf", "blk", None, None),
        P(("leaf", "blk"), None),
        P(("leaf", "blk"), None),
        P(("leaf", "blk"), None),
        P(),
        P(),
        P(),
        P(),
    )
    out_specs = (P(None, ("leaf", "blk"), None), P(None, ("leaf", "blk"), None))
    return jax.shard_map(shards, mesh=mesh, in_specs=in_specs, out_specs=out_specs, check_vma=False)
```

```python
import functools

import jax
import jax.numpy as jnp
from jax import lax
from jax.experimental import pallas as pl
from jax.experimental.pallas import tpu as pltpu
from jax.sharding import PartitionSpec as P

BF16 = jnp.bfloat16
F32 = jnp.float32
MIB = 1024 * 1024
SMEM = pl.BlockSpec(memory_space=pltpu.SMEM)
VMEM = pl.BlockSpec(memory_space=pltpu.VMEM)


def near_of(lane):
    return lane ^ (2 + 4 * (lane & 1))


def core_of():
    return lax.axis_index("blk") & 1


def side_of():
    return lax.axis_index("blk") >> 1 & 1


def node_of(level):
    return lax.axis_index("leaf") // (lax.axis_size("leaf") >> level)


def live(node_blocks, level, lane):
    leaf = lax.axis_index("leaf") % (lax.axis_size("leaf") >> level)
    position = leaf * lax.axis_size("blk") + lane
    limit = node_blocks[2**level - 1 + node_of(level)]
    return jnp.where(position < limit, 1.0, 0.0).astype(F32)


def call(kernel, name, out_shape, smem, vmem, scratch=(), limit=24):
    return pl.pallas_call(
        kernel,
        out_shape=out_shape,
        in_specs=[SMEM] * len(smem) + [VMEM] * len(vmem),
        out_specs=jax.tree.map(lambda _: VMEM, out_shape),
        scratch_shapes=list(scratch),
        compiler_params=pltpu.CompilerParams(vmem_limit_bytes=limit * MIB),
        name=name,
    )(*smem, *vmem)


def array(*shape, dtype=BF16):
    return jax.ShapeDtypeStruct(shape, dtype)


def total_of(parts):
    total = parts[0].astype(F32)
    for part in parts[1:]:
        total = total + part.astype(F32)
    return total


def first_kernel(loads, out):
    lower = loads[2].astype(BF16)
    middle, root = loads[1].astype(BF16).T, loads[0].astype(BF16).T
    for chip in range(out.shape[0]):
        side = (chip & 1) * 64
        out[chip, :128, :] = lower
        out[chip, 128:192, :] = middle[side : side + 64]
        out[chip, 192:256, :] = root[side : side + 64]


def multiply_kernel(transposed, own, other, tile, out, columns):
    first = core_of() == 0
    for chip in range(own.shape[0]):
        mine, theirs = own[chip], other[chip]
        for core in range(2):
            block = jnp.where(first == (core == 0), mine, theirs)
            row = (2 * chip + core) * 128
            columns[row : row + 128, :] = block.T if transposed else block
    for group in range(out.shape[0]):
        rows = tile[group * 128 : group * 128 + 128, :]
        product = jnp.dot(rows, columns[...], preferred_element_type=F32)
        out[group] = product.astype(BF16).T


def multiply(own, other, tile, transposed):
    return call(
        functools.partial(multiply_kernel, transposed),
        "multiply",
        array(tile.shape[0] // 128, 128, 128),
        [],
        [own, other, tile],
        [pltpu.VMEM((tile.shape[1], 128), BF16)],
    )


def transposed_kernel(gathered, tile, mine, theirs):
    first = core_of() == 0
    rows = jnp.concatenate([gathered[a] for a in range(gathered.shape[0])], axis=1)
    for chip in range(mine.shape[0]):
        column = chip * 256
        product = jnp.dot(rows, tile[:, column : column + 256], preferred_element_type=F32)
        even, odd = product[:, :128], product[:, 128:]
        mine[chip] = jnp.where(first, even, odd)
        theirs[chip] = jnp.where(first, odd, even).astype(BF16)


def multiply_transposed(gathered, tile):
    chips = tile.shape[1] // 256
    return call(
        transposed_kernel,
        "multiply_transposed",
        (array(chips, 128, 128, dtype=F32), array(chips, 128, 128)),
        [],
        [gathered, tile],
    )


def lift_kernel(spans, levels, node_blocks, *refs):
    total = len(spans)
    patterns, refs = refs[:total], refs[total:]
    parts, refs = refs[0], refs[1:]
    earlier, refs = refs[: total - 1], refs[total - 1 :]
    factors, (solved, keep, send, sums) = refs[: 2 * total], refs[2 * total :]
    core, side = core_of(), side_of()
    lane = lax.axis_index("blk")
    half = keep.shape[0]
    for place in range(2):
        which = side if place == 0 else 1 - side
        summed = total_of([parts[g, which] for g in range(parts.shape[0])])
        factor = live(node_blocks, levels[0], near_of(lane) if place else lane)
        solved[place] = (summed * factor).astype(BF16)
    values = [jnp.concatenate([s[0], s[1]], axis=1) for s in (solved, *earlier)]
    sums[...] = jnp.zeros_like(sums)
    for index, span in enumerate(spans):
        node = node_of(levels[index])
        own, near = factors[2 * index], factors[2 * index + 1]

        def chunk(step, carry, index=index, node=node, own=own, near=near):
            columns = pl.ds(pl.multiple_of(step * 1024, 1024), 1024)
            factor = jnp.concatenate([own[:, columns], near[:, columns]], axis=0)
            product = jnp.dot(values[index], factor, preferred_element_type=F32)
            for part in range(8):
                block = patterns[index][node, step * 8 + part]
                slot = ((block & 1) ^ core) * half + (block >> 1)
                sums[slot] += product[:, part * 128 : part * 128 + 128]
            return carry

        lax.fori_loop(0, span // 1024, chunk, 0)

    def emit(slot, carry):
        keep[slot] = sums[slot].astype(BF16)
        send[slot] = sums[half + slot].astype(BF16)
        return carry

    lax.fori_loop(0, half, emit, 0, unroll=4)


def lift(node_blocks, levels, patterns, parts, earlier, factors, half):
    spans = tuple(f.shape[1] for f in factors[::2])
    return call(
        functools.partial(lift_kernel, spans, levels),
        "lift",
        (array(2, 64, 128), array(half, 64, 128), array(half, 64, 128)),
        [node_blocks, *patterns],
        [parts, *earlier, *factors],
        [pltpu.VMEM((2 * half, 64, 128), F32)],
    )


def rest_kernel(parts, load, copies):
    chip, near = lax.axis_index("blk") >> 1, near_of(lax.axis_index("blk")) >> 1
    for place in range(parts.shape[1]):
        total = total_of([parts[g, place] for g in range(parts.shape[0])])
        given = (chip == place) | (near == place)
        value = (jnp.where(given, load[place].astype(F32), 0.0) - total).astype(BF16)
        for index in range(copies.shape[0]):
            copies[index, place] = value


def join_kernel(parts, out):
    for place in range(out.shape[0]):
        for side in range(2):
            total = parts[side, place].astype(F32) + parts[2 + side, place].astype(F32)
            out[place, side * 64 : side * 64 + 64, :] = total.astype(BF16)


def split_kernel(mine, theirs, out):
    for place in range(mine.shape[0]):
        value = (mine[place] + theirs[place].astype(F32)).astype(BF16)
        for chip in range(out.shape[0]):
            side = (chip & 1) * 64
            out[chip, place] = value[side : side + 64]


def spread_kernel(level, node_blocks, parts, own, near, copies):
    lane = lax.axis_index("blk")
    for place in range(parts.shape[1]):
        value = total_of([parts[x, place] for x in range(parts.shape[0])])
        if level:
            value = value * live(node_blocks, level, 2 * place + (lane & 1))
        value = value.astype(BF16)

        @pl.when(lane >> 1 == place)
        def _():
            own[...] = value

        @pl.when(near_of(lane) >> 1 == place)
        def _():
            near[...] = value

        for index in range(copies.shape[0]):
            copies[index, place] = value


def root_kernel(parts, solved, copies):
    value = total_of([parts[g] for g in range(parts.shape[0])]).astype(BF16)
    solved[...] = value
    for index in range(copies.shape[0]):
        copies[index] = value


def pulled_of(level, pattern, own, other, factor, near, chosen):
    core, row_of = core_of(), node_of(level)

    def pick(position, carry):
        block = pattern[row_of, position]
        mine = (block & 1) == core
        column = pl.multiple_of(position * 128, 128)
        chosen[:, pl.ds(column, 128)] = jnp.where(mine, own[block >> 1], other[block >> 1])
        return carry

    lax.fori_loop(0, pattern.shape[1], pick, 0, unroll=4)
    result = []
    for rows in (factor, near):
        product = lax.dot_general(
            rows[...], chosen[...], (((1,), (1,)), ((), ())), preferred_element_type=F32
        )
        result.append(product.T)
    return result


def pull_kernel(level, pattern, own, other, factor, near, out, chosen):
    out[0], out[1] = pulled_of(level, pattern, own, other, factor, near, chosen)


def reduce_kernel(level, pattern, own, other, factor, near, solved, *refs):
    earlier, (copies, chosen) = refs[:-2], refs[-2:]
    side = side_of()
    pulled = pulled_of(level, pattern, own, other, factor, near, chosen)
    for place in range(2):
        value = pulled[place]
        for e in earlier:
            value = value + e[place]
        value = (solved[place].astype(F32) - value).astype(BF16)
        which = side if place == 0 else 1 - side
        for index in range(copies.shape[0]):
            copies[index, which] = value


def pull(level, pattern, own, other, factors):
    return call(
        functools.partial(pull_kernel, level),
        "pull",
        array(2, 64, 128, dtype=F32),
        [pattern],
        [own, other, *factors],
        [pltpu.VMEM((64, factors[0].shape[1]), BF16)],
    )


def reduced(level, pattern, own, other, factors, solved, earlier, count):
    return call(
        functools.partial(reduce_kernel, level),
        "reduced",
        array(count, 2, 64, 128),
        [pattern],
        [own, other, *factors, solved, *earlier],
        [pltpu.VMEM((64, factors[0].shape[1]), BF16)],
    )


def whole(mine, far):
    first = side_of() == 0
    low, high = jnp.where(first, mine, far), jnp.where(first, far, mine)
    return jnp.concatenate([low, high], axis=0).T


def stack_kernel(root, middle, lower, far, out):
    out[0] = root[...].T
    out[1] = whole(middle[0], far[2])
    out[2] = whole(lower[0], far[3])


def last_kernel(node_blocks, parts, root, middle, far, out):
    out[0] = whole(root[...], far[0])
    out[1] = whole(middle[...], far[1])
    total = total_of([parts[x] for x in range(parts.shape[0])])
    out[2] = (total * live(node_blocks, 2, lax.axis_index("blk"))).astype(BF16).T


def shards(
    loads,
    inverse_root,
    inverse_middle,
    inverse_lower,
    couple_middle,
    couple_lower,
    couple_between,
    pattern_middle,
    pattern_lower,
    pattern_between,
    node_blocks,
):
    leaf_count = lax.axis_size("leaf")
    block_count = lax.axis_size("blk")
    chip_count = block_count // 2
    chip_groups = [[2 * x + c for x in range(chip_count)] for c in range(2)]
    even_lanes = [i for i in range(block_count) if i >> 1 & 1 == 0]

    def leaf_groups(level):
        size = leaf_count >> level
        return [[g * size + j for j in range(size)] for g in range(1 << level)]

    def pair_groups(level):
        return [
            [leaf * block_count + i for leaf in group for i in (lane, near_of(lane))]
            for group in leaf_groups(level)
            for lane in even_lanes
        ]

    def swap_core(value):
        return lax.ppermute(value, "blk", [(i, i ^ 1) for i in range(block_count)])

    def swap_near(value):
        return lax.ppermute(value, "blk", [(i, near_of(i)) for i in range(block_count)])

    kept = {}

    def fence(value):
        tied, held = lax.optimization_barrier((value, dict(kept)))
        kept.update(held)
        return tied

    def exchange(value, axis, groups):
        value = fence(value)
        value = lax.all_to_all(value, axis, 0, 0, tiled=True, axis_index_groups=groups)
        return fence(value)

    def over_chips(value):
        return exchange(value, "blk", chip_groups)

    def over_leaf(value, level):
        return exchange(value, "leaf", leaf_groups(level) if level else None)

    def over_pair(value, level):
        size = leaf_count >> level
        value = exchange(value.reshape(2 * size, 64, 128), ("leaf", "blk"), pair_groups(level))
        return value.reshape(size, 2, 64, 128)

    halves = array(chip_count, chip_count, 64, 128)

    def residual(load, level, before_chips=lambda: None):
        size = leaf_count >> level
        keep, send = kept.pop("keep"), kept.pop("send")
        summed = (keep.astype(F32) + swap_core(send).astype(F32)).astype(BF16)
        parts = over_leaf(summed.reshape(size, chip_count, 64, 128), level)
        before_chips()
        parts = over_chips(call(rest_kernel, "rest", halves, [], [parts, kept.pop(load)]))
        rest = call(join_kernel, "join", array(chip_count, 128, 128), [], [parts])
        return rest, swap_core(rest)

    def backward(gathered, tile):
        mine, theirs = multiply_transposed(gathered, tile)
        return mine, swap_core(theirs)

    def spread(partial_sums, level):
        size = leaf_count >> level
        parts = over_chips(call(split_kernel, "split", halves, [], partial_sums))
        own, near, copies = call(
            functools.partial(spread_kernel, level), "spread",
            (array(64, 128), array(64, 128), array(size, chip_count, 64, 128)),
            [node_blocks], [parts],
        )
        kept[f"own{level}"], kept[f"near{level}"] = own, near
        blocks = over_leaf(copies, level).reshape(-1, 64, 128)
        return blocks, swap_core(blocks)

    tile_root, tile_middle, tile_lower = inverse_root[0, 0], inverse_middle[0, 0], inverse_lower[0, 0]
    kept["couples"] = [couple_between, couple_lower, couple_middle]

    loaded = over_chips(call(first_kernel, "first", array(chip_count, 256, 128), [], [loads]))
    between = [couple_between, swap_near(kept["couples"][0])]
    own = loaded[:, :128]
    kept["load_middle"], kept["load_root"] = loaded[:, 128:192], loaded[:, 192:]
    parts = over_pair(multiply(own, swap_core(own), tile_lower, False), 2)
    lower = [couple_lower, swap_near(kept["couples"][1])]
    kept["y_lower"], kept["keep"], kept["send"] = lift(
        node_blocks, (2,), [pattern_between], parts, [], between, (leaf_count >> 1) * chip_count
    )
    def before_chips():
        kept["lower"] = lower[1]

    own, other = residual("load_middle", 1, before_chips)
    middle = [couple_middle, swap_near(kept.pop("couples")[2])]
    lower[1] = kept.pop("lower")
    parts = over_pair(multiply(own, other, tile_middle, True), 1)
    kept["y_middle"], kept["keep"], kept["send"] = lift(
        node_blocks, (1, 2), [pattern_middle, pattern_lower], parts, [kept["y_lower"]],
        middle + lower, leaf_count * chip_count,
    )
    own, other = residual("load_root", 0)
    parts = over_leaf(multiply(own, other, tile_root, True), 0)
    kept["y_root"], copies = call(
        root_kernel, "root", (array(128, 128), array(leaf_count, 128, 128)), [], [parts]
    )
    own, other = spread(backward(over_leaf(copies, 0), tile_root), 0)
    copies = reduced(
        1, pattern_middle, own, other, middle, kept["y_middle"], [], leaf_count >> 1
    )
    kept["own_root"], kept["other_root"] = own, other
    gathered = over_pair(copies, 1).reshape(-1, 128, 128)
    own, other = spread(backward(gathered, tile_middle), 1)
    pulled = pull(2, pattern_lower, kept.pop("own_root"), kept.pop("other_root"), lower)
    copies = reduced(
        2, pattern_between, own, other, between, kept["y_lower"], [pulled], leaf_count >> 2
    )
    kept["far"] = swap_near(
        jnp.stack([kept.pop("near0"), kept.pop("near1"), kept["y_middle"][1], kept["y_lower"][1]])
    )
    gathered = over_pair(copies, 2).reshape(-1, 128, 128)
    mine, theirs = backward(gathered, tile_lower)
    kept["forward"] = call(
        stack_kernel, "stack", array(3, 128, 128), [],
        [kept.pop("y_root"), kept.pop("y_middle"), kept.pop("y_lower"), kept["far"]],
    )
    parts = over_chips((mine + theirs.astype(F32)).astype(BF16))
    answer = call(
        last_kernel, "last", array(3, 128, 128), [node_blocks],
        [parts, kept["own0"], kept["own1"], kept["far"]],
    )
    return (kept["forward"], answer)


def solution(mesh):
    in_specs = (
        P(None, ("leaf", "blk"), None),
        P("leaf", "blk", None, None),
        P("leaf", "blk", None, None),
        P("leaf", "blk", None, None),
        P(("leaf", "blk"), None),
        P(("leaf", "blk"), None),
        P(("leaf", "blk"), None),
        P(),
        P(),
        P(),
        P(),
    )
    out_specs = (P(None, ("leaf", "blk"), None), P(None, ("leaf", "blk"), None))
    return jax.shard_map(shards, mesh=mesh, in_specs=in_specs, out_specs=out_specs, check_vma=False)
```

```python
import functools

import jax
import jax.numpy as jnp
from jax import lax
from jax.experimental import pallas as pl
from jax.experimental.pallas import tpu as pltpu
from jax.sharding import PartitionSpec as P

BF16 = jnp.bfloat16
F32 = jnp.float32
MIB = 1024 * 1024
SMEM = pl.BlockSpec(memory_space=pltpu.SMEM)
VMEM = pl.BlockSpec(memory_space=pltpu.VMEM)


def near_of(lane):
    return lane ^ (2 + 4 * (lane & 1))


def core_of():
    return lax.axis_index("blk") & 1


def side_of():
    return lax.axis_index("blk") >> 1 & 1


def node_of(level):
    return lax.axis_index("leaf") // (lax.axis_size("leaf") >> level)


def leaf_near_of(leaf, lane):
    return leaf ^ (1 + 2 * (lane & 1))


def live(node_blocks, level, lane, leaf=None):
    leaf = lax.axis_index("leaf") if leaf is None else leaf
    leaf = leaf % (lax.axis_size("leaf") >> level)
    position = leaf * lax.axis_size("blk") + lane
    limit = node_blocks[2**level - 1 + node_of(level)]
    return jnp.where(position < limit, 1.0, 0.0).astype(F32)


def call(kernel, name, out_shape, smem, vmem, scratch=(), limit=24):
    return pl.pallas_call(
        kernel,
        out_shape=out_shape,
        in_specs=[SMEM] * len(smem) + [VMEM] * len(vmem),
        out_specs=jax.tree.map(lambda _: VMEM, out_shape),
        scratch_shapes=list(scratch),
        compiler_params=pltpu.CompilerParams(vmem_limit_bytes=limit * MIB),
        name=name,
    )(*smem, *vmem)


def array(*shape, dtype=BF16):
    return jax.ShapeDtypeStruct(shape, dtype)


def total_of(parts):
    total = parts[0].astype(F32)
    for part in parts[1:]:
        total = total + part.astype(F32)
    return total


def first_kernel(loads, out):
    lower, root = loads[2].astype(BF16), loads[0].astype(BF16).T
    for chip in range(out.shape[0]):
        side = (chip & 1) * 64
        out[chip, :128, :] = lower
        out[chip, 128:192, :] = root[side : side + 64]


def gather_columns(transposed, own, other, columns):
    first = core_of() == 0
    for chip in range(own.shape[0]):
        mine, theirs = own[chip], other[chip]
        for core in range(2):
            block = jnp.where(first == (core == 0), mine, theirs)
            row = (2 * chip + core) * 128
            columns[row : row + 128, :] = block.T if transposed else block


def partial_of(tile, columns, group):
    rows = tile[group * 128 : group * 128 + 128, :]
    return jnp.dot(rows, columns[...], preferred_element_type=F32).astype(BF16).T


def multiply_kernel(own, other, tile, out, columns):
    gather_columns(True, own, other, columns)
    for group in range(out.shape[0]):
        out[group] = partial_of(tile, columns, group)


def multiply_lower_kernel(own, other, tile, out, columns):
    gather_columns(False, own, other, columns)
    partials = [partial_of(tile, columns, group) for group in range(out.shape[0])]
    first = core_of() == 0
    for group in range(out.shape[0]):
        near = jnp.where(first, partials[group ^ 1], partials[group ^ 3])
        side = (group & 1) * 64
        out[group, :128, :] = partials[group]
        out[group, 128:, :] = near[side : side + 64]


def multiply(kernel, rows, own, other, tile):
    return call(
        kernel,
        "multiply",
        array(tile.shape[0] // 128, rows, 128),
        [],
        [own, other, tile],
        [pltpu.VMEM((tile.shape[1], 128), BF16)],
    )


def transposed_kernel(gathered, tile, mine, theirs):
    first = core_of() == 0
    rows = jnp.concatenate([gathered[a] for a in range(gathered.shape[0])], axis=1)
    for chip in range(mine.shape[0]):
        column = chip * 256
        product = jnp.dot(rows, tile[:, column : column + 256], preferred_element_type=F32)
        even, odd = product[:, :128], product[:, 128:]
        mine[chip] = jnp.where(first, even, odd)
        theirs[chip] = jnp.where(first, odd, even).astype(BF16)


def multiply_transposed(gathered, tile):
    chips = tile.shape[1] // 256
    return call(
        transposed_kernel,
        "multiply_transposed",
        (array(chips, 128, 128, dtype=F32), array(chips, 128, 128)),
        [],
        [gathered, tile],
    )


def place_updates(spans, levels, patterns, values, factors, keep, send, sums):
    core = core_of()
    half = keep.shape[0]
    sums[...] = jnp.zeros_like(sums)
    for index, span in enumerate(spans):
        node = node_of(levels[index])

        def chunk(step, carry, index=index, node=node):
            columns = pl.ds(pl.multiple_of(step * 1024, 1024), 1024)
            factor = jnp.concatenate([f[:, columns] for f in factors[index]], axis=0)
            product = jnp.dot(values[index], factor, preferred_element_type=F32)
            for part in range(8):
                block = patterns[index][node, step * 8 + part]
                slot = ((block & 1) ^ core) * half + (block >> 1)
                sums[slot] += product[:, part * 128 : part * 128 + 128]
            return carry

        lax.fori_loop(0, span // 1024, chunk, 0)

    def emit(slot, carry):
        keep[slot] = sums[slot].astype(BF16)
        send[slot] = sums[half + slot].astype(BF16)
        return carry

    lax.fori_loop(0, half, emit, 0, unroll=4)


def lower_kernel(node_blocks, pattern, parts, factor, near, solved, own, far, keep, send, sums):
    leaf, lane = lax.axis_index("leaf"), lax.axis_index("blk")
    total = total_of([parts[g, :128, :] for g in range(parts.shape[0])])
    value = (total * live(node_blocks, 2, lane)).astype(BF16)
    total = total_of([parts[g, 128:, :] for g in range(parts.shape[0])])
    partner = (total * live(node_blocks, 2, lane, leaf_near_of(leaf, lane))).astype(BF16)
    solved[...] = value
    first = side_of() == 0
    low, high = value[:64], value[64:]
    own[...] = jnp.where(first, low, high)
    far[...] = jnp.where(first, high, low)
    values = jnp.concatenate([jnp.where(leaf & 1 == 0, low, high), partner], axis=1)
    spans = (factor.shape[1],)
    place_updates(spans, (2,), [pattern], [values], [[factor, near]], keep, send, sums)


def pair_kernel(node_blocks, pattern, pattern_lower, parts, lower, lower_near, *refs):
    factors, (solved, keep, send, sums) = refs[:4], refs[4:]
    side, lane = side_of(), lax.axis_index("blk")
    for place in range(2):
        which = side if place == 0 else 1 - side
        total = total_of([parts[g, which] for g in range(parts.shape[0])])
        factor = live(node_blocks, 1, near_of(lane) if place else lane)
        solved[place] = (total * factor).astype(BF16)
    values = [
        jnp.concatenate([solved[0], solved[1]], axis=1),
        jnp.concatenate([lower[...], lower_near[...]], axis=1),
    ]
    spans = (factors[0].shape[1], factors[2].shape[1])
    place_updates(
        spans, (1, 2), [pattern, pattern_lower], values, [factors[:2], factors[2:]],
        keep, send, sums,
    )


def rest_kernel(parts, load, copies):
    chip, near = lax.axis_index("blk") >> 1, near_of(lax.axis_index("blk")) >> 1
    for place in range(parts.shape[1]):
        total = total_of([parts[g, place] for g in range(parts.shape[0])])
        given = (chip == place) | (near == place)
        value = (jnp.where(given, load[place].astype(F32), 0.0) - total).astype(BF16)
        for index in range(copies.shape[0]):
            copies[index, place] = value


def rest_middle_kernel(parts, loads, far, copies):
    chip = lax.axis_index("blk") >> 1
    load = loads[1].T
    for place in range(parts.shape[1]):
        total = [total_of([parts[g, place] for g in range(y, parts.shape[0], 2)]) for y in range(2)]
        total = jnp.concatenate(total, axis=0)
        value = (jnp.where(chip == place, load, 0.0) - total).astype(BF16)
        for index in range(copies.shape[0]):
            copies[index, place * 128 : place * 128 + 128, :] = value
    for index in range(copies.shape[0]):
        copies[index, parts.shape[1] * 128 :, :] = far[...]


def join_middle_kernel(parts, out, near):
    for place in range(out.shape[0]):
        rows = pl.ds(place * 128, 128)
        out[place] = total_of([parts[x, rows, :] for x in range(parts.shape[0])]).astype(BF16)
    near[...] = parts[near_of(lax.axis_index("blk")) >> 1, out.shape[0] * 128 :, :]


def join_kernel(parts, out):
    for place in range(out.shape[0]):
        for side in range(2):
            total = parts[side, place].astype(F32) + parts[2 + side, place].astype(F32)
            out[place, side * 64 : side * 64 + 64, :] = total.astype(BF16)


def split_kernel(mine, theirs, out):
    for place in range(mine.shape[0]):
        value = (mine[place] + theirs[place].astype(F32)).astype(BF16)
        for chip in range(out.shape[0]):
            side = (chip & 1) * 64
            out[chip, place] = value[side : side + 64]


def spread_kernel(level, node_blocks, parts, own, near, copies):
    lane = lax.axis_index("blk")
    for place in range(parts.shape[1]):
        value = total_of([parts[x, place] for x in range(parts.shape[0])])
        if level:
            value = value * live(node_blocks, level, 2 * place + (lane & 1))
        value = value.astype(BF16)

        @pl.when(lane >> 1 == place)
        def _():
            own[...] = value

        @pl.when(near_of(lane) >> 1 == place)
        def _():
            near[...] = value

        for index in range(copies.shape[0]):
            copies[index, place] = value


def root_kernel(parts, solved, copies):
    value = total_of([parts[g] for g in range(parts.shape[0])]).astype(BF16)
    solved[...] = value
    for index in range(copies.shape[0]):
        copies[index] = value


def pulled_of(level, pattern, own, other, factor, near, chosen):
    core, row_of = core_of(), node_of(level)

    def pick(position, carry):
        block = pattern[row_of, position]
        mine = (block & 1) == core
        column = pl.multiple_of(position * 128, 128)
        chosen[:, pl.ds(column, 128)] = jnp.where(mine, own[block >> 1], other[block >> 1])
        return carry

    lax.fori_loop(0, pattern.shape[1], pick, 0, unroll=4)
    result = []
    for rows in (factor, near):
        product = lax.dot_general(
            rows[...], chosen[...], (((1,), (1,)), ((), ())), preferred_element_type=F32
        )
        result.append(product.T)
    return result


def pull_kernel(level, pattern, own, other, factor, near, out, chosen):
    out[0], out[1] = pulled_of(level, pattern, own, other, factor, near, chosen)


def reduce_kernel(level, pattern, own, other, factor, near, solved, *refs):
    earlier, (copies, chosen) = refs[:-2], refs[-2:]
    side = side_of()
    pulled = pulled_of(level, pattern, own, other, factor, near, chosen)
    for place in range(2):
        value = pulled[place]
        for e in earlier:
            value = value + e[place]
        value = (solved[place].astype(F32) - value).astype(BF16)
        which = side if place == 0 else 1 - side
        for index in range(copies.shape[0]):
            copies[index, which] = value


def pull(level, pattern, own, other, factors):
    return call(
        functools.partial(pull_kernel, level),
        "pull",
        array(2, 64, 128, dtype=F32),
        [pattern],
        [own, other, *factors],
        [pltpu.VMEM((64, factors[0].shape[1]), BF16)], 12,
    )


def reduced(level, pattern, own, other, factors, solved, earlier, count):
    return call(
        functools.partial(reduce_kernel, level),
        "reduced",
        array(count, 2, 64, 128),
        [pattern],
        [own, other, *factors, solved, *earlier],
        [pltpu.VMEM((64, factors[0].shape[1]), BF16)], 12,
    )


def whole(mine, far):
    first = side_of() == 0
    low, high = jnp.where(first, mine, far), jnp.where(first, far, mine)
    return jnp.concatenate([low, high], axis=0).T


def stack_kernel(root, middle, lower, far, out):
    out[0] = root[...].T
    out[1] = whole(middle[0], far[2])
    out[2] = lower[...].T


def last_kernel(node_blocks, parts, root, middle, far, out):
    out[0] = whole(root[...], far[0])
    out[1] = whole(middle[...], far[1])
    total = total_of([parts[x] for x in range(parts.shape[0])])
    out[2] = (total * live(node_blocks, 2, lax.axis_index("blk"))).astype(BF16).T


def shards(
    loads,
    inverse_root,
    inverse_middle,
    inverse_lower,
    couple_middle,
    couple_lower,
    couple_between,
    pattern_middle,
    pattern_lower,
    pattern_between,
    node_blocks,
):
    leaf_count = lax.axis_size("leaf")
    block_count = lax.axis_size("blk")
    chip_count = block_count // 2
    chip_groups = [[2 * x + c for x in range(chip_count)] for c in range(2)]
    even_lanes = [i for i in range(block_count) if i >> 1 & 1 == 0]

    def leaf_groups(level):
        size = leaf_count >> level
        return [[g * size + j for j in range(size)] for g in range(1 << level)]

    def pair_groups(level):
        return [
            [leaf * block_count + i for leaf in group for i in (lane, near_of(lane))]
            for group in leaf_groups(level)
            for lane in even_lanes
        ]

    def swap_core(value):
        return lax.ppermute(value, "blk", [(i, i ^ 1) for i in range(block_count)])

    def swap_near(value):
        return lax.ppermute(value, "blk", [(i, near_of(i)) for i in range(block_count)])

    def swap_leaf_near(value):
        pairs = []
        for i in range(leaf_count * block_count):
            leaf, lane = divmod(i, block_count)
            pairs.append((i, leaf_near_of(leaf, lane) * block_count + lane))
        return lax.ppermute(value, ("leaf", "blk"), pairs)

    kept = {}

    def fence(value):
        tied, held = lax.optimization_barrier((value, dict(kept)))
        kept.update(held)
        return tied

    def exchange(value, axis, groups):
        value = fence(value)
        value = lax.all_to_all(value, axis, 0, 0, tiled=True, axis_index_groups=groups)
        return fence(value)

    def over_chips(value):
        return exchange(value, "blk", chip_groups)

    def over_leaf(value, level):
        return exchange(value, "leaf", leaf_groups(level) if level else None)

    def over_pair(value, level):
        size = leaf_count >> level
        value = exchange(value.reshape(2 * size, 64, 128), ("leaf", "blk"), pair_groups(level))
        return value.reshape(size, 2, 64, 128)

    halves = array(chip_count, chip_count, 64, 128)

    def updates(keep, send, level):
        summed = (keep.astype(F32) + swap_core(send).astype(F32)).astype(BF16)
        size = leaf_count >> level
        return over_leaf(summed.reshape((size, chip_count) + keep.shape[1:]), level)

    def backward(gathered, tile):
        mine, theirs = multiply_transposed(gathered, tile)
        return mine, swap_core(theirs)

    def spread(partial_sums, level):
        size = leaf_count >> level
        parts = over_chips(call(split_kernel, "split", halves, [], partial_sums))
        own, near, copies = call(
            functools.partial(spread_kernel, level), "spread",
            (array(64, 128), array(64, 128), array(size, chip_count, 64, 128)),
            [node_blocks], [parts],
        )
        kept[f"own{level}"], kept[f"near{level}"] = own, near
        blocks = over_leaf(copies, level).reshape(-1, 64, 128)
        return blocks, swap_core(blocks)

    tile_root, tile_middle, tile_lower = inverse_root[0, 0], inverse_middle[0, 0], inverse_lower[0, 0]
    leaf_near_between = swap_leaf_near(couple_between)
    kept["couples"] = [couple_between, couple_lower, couple_middle]

    loaded = over_chips(call(first_kernel, "first", array(chip_count, 192, 128), [], [loads]))
    lower = [couple_lower, swap_near(kept["couples"][1])]
    middle = [couple_middle, swap_near(kept["couples"][2])]
    own = loaded[:, :128]
    kept["load_root"] = loaded[:, 128:]
    parts = over_leaf(multiply(multiply_lower_kernel, 192, own, swap_core(own), tile_lower), 2)
    half = (leaf_count >> 1) * chip_count
    parts, lower[1] = lax.optimization_barrier((parts, lower[1]))
    y_lower, own, far, keep, send = call(
        lower_kernel, "lift_lower",
        (array(128, 128), array(64, 128), array(64, 128), array(half, 64, 128), array(half, 64, 128)),
        [node_blocks, pattern_between], [parts, couple_between, leaf_near_between],
        [pltpu.VMEM((2 * half, 64, 128), F32)],
    )
    kept["y_lower"], kept["y_lower_own"], kept["far"], kept["lower"] = y_lower, own, far, lower[1]
    parts = updates(keep, send, 1)
    kept["middle"] = middle[1]
    rows = chip_count * 128 + 64
    parts = over_chips(
        call(
            rest_middle_kernel, "rest", array(chip_count, rows, 128), [],
            [parts, loads, kept.pop("far")],
        )
    )
    own, kept["y_lower_near"] = call(
        join_middle_kernel, "join", (array(chip_count, 128, 128), array(64, 128)), [], [parts]
    )
    parts = over_pair(multiply(multiply_kernel, 128, own, swap_core(own), tile_middle), 1)
    lower[1], middle[1] = kept.pop("lower"), kept.pop("middle")
    near_between = swap_near(kept.pop("couples")[0])
    half = leaf_count * chip_count
    kept["y_middle"], keep, send = call(
        pair_kernel, "lift_pair",
        (array(2, 64, 128), array(half, 64, 128), array(half, 64, 128)),
        [node_blocks, pattern_middle, pattern_lower],
        [parts, kept["y_lower_own"], kept["y_lower_near"], *middle, *lower],
        [pltpu.VMEM((2 * half, 64, 128), F32)], 16,
    )
    parts = updates(keep, send, 0)
    kept["near_between"] = near_between
    parts = over_chips(call(rest_kernel, "rest", halves, [], [parts, kept.pop("load_root")]))
    own = call(join_kernel, "join", array(chip_count, 128, 128), [], [parts])
    parts = over_leaf(multiply(multiply_kernel, 128, own, swap_core(own), tile_root), 0)
    kept["y_root"], copies = call(
        root_kernel, "root", (array(128, 128), array(leaf_count, 128, 128)), [], [parts]
    )
    own, other = spread(backward(over_leaf(copies, 0), tile_root), 0)
    copies = reduced(
        1, pattern_middle, own, other, middle, kept["y_middle"], [], leaf_count >> 1
    )
    kept["own_root"], kept["other_root"] = own, other
    gathered = over_pair(copies, 1).reshape(-1, 128, 128)
    own, other = spread(backward(gathered, tile_middle), 1)
    pulled = pull(2, pattern_lower, kept.pop("own_root"), kept.pop("other_root"), lower)
    between = [couple_between, kept.pop("near_between")]
    solved = jnp.stack([kept.pop("y_lower_own"), kept.pop("y_lower_near")])
    copies = reduced(2, pattern_between, own, other, between, solved, [pulled], leaf_count >> 2)
    kept["far"] = swap_near(
        jnp.stack([kept.pop("near0"), kept.pop("near1"), kept["y_middle"][1]])
    )
    gathered = over_pair(copies, 2).reshape(-1, 128, 128)
    mine, theirs = backward(gathered, tile_lower)
    kept["forward"] = call(
        stack_kernel, "stack", array(3, 128, 128), [],
        [kept.pop("y_root"), kept.pop("y_middle"), kept.pop("y_lower"), kept["far"]],
    )
    parts = over_chips((mine + theirs.astype(F32)).astype(BF16))
    answer = call(
        last_kernel, "last", array(3, 128, 128), [node_blocks],
        [parts, kept["own0"], kept["own1"], kept["far"]],
    )
    return (kept["forward"], answer)


def solution(mesh):
    in_specs = (
        P(None, ("leaf", "blk"), None),
        P("leaf", "blk", None, None),
        P("leaf", "blk", None, None),
        P("leaf", "blk", None, None),
        P(("leaf", "blk"), None),
        P(("leaf", "blk"), None),
        P(("leaf", "blk"), None),
        P(),
        P(),
        P(),
        P(),
    )
    out_specs = (P(None, ("leaf", "blk"), None), P(None, ("leaf", "blk"), None))
    return jax.shard_map(shards, mesh=mesh, in_specs=in_specs, out_specs=out_specs, check_vma=False)
```

```python
import functools

import jax
import jax.numpy as jnp
from jax import lax
from jax.experimental import pallas as pl
from jax.experimental.pallas import tpu as pltpu
from jax.sharding import PartitionSpec as P

BF16 = jnp.bfloat16
F32 = jnp.float32
MIB = 1024 * 1024
SMEM = pl.BlockSpec(memory_space=pltpu.SMEM)
VMEM = pl.BlockSpec(memory_space=pltpu.VMEM)


def near_of(lane):
    return lane ^ (2 + 4 * (lane & 1))


def core_of():
    return lax.axis_index("blk") & 1


def side_of():
    return lax.axis_index("blk") >> 1 & 1


def node_of(level):
    return lax.axis_index("leaf") // (lax.axis_size("leaf") >> level)


def leaf_near_of(leaf, lane):
    return leaf ^ (1 + 2 * (lane & 1))


def live(node_blocks, level, lane, leaf=None):
    leaf = lax.axis_index("leaf") if leaf is None else leaf
    leaf = leaf % (lax.axis_size("leaf") >> level)
    position = leaf * lax.axis_size("blk") + lane
    limit = node_blocks[2**level - 1 + node_of(level)]
    return jnp.where(position < limit, 1.0, 0.0).astype(F32)


def call(kernel, name, out_shape, smem, vmem, scratch=(), limit=24, cost=None):
    return pl.pallas_call(
        kernel,
        out_shape=out_shape,
        in_specs=[SMEM] * len(smem) + [VMEM] * len(vmem),
        out_specs=jax.tree.map(lambda _: VMEM, out_shape),
        scratch_shapes=list(scratch),
        compiler_params=pltpu.CompilerParams(vmem_limit_bytes=limit * MIB),
        cost_estimate=cost,
        name=name,
    )(*smem, *vmem)


def array(*shape, dtype=BF16):
    return jax.ShapeDtypeStruct(shape, dtype)


def total_of(parts):
    total = parts[0].astype(F32)
    for part in parts[1:]:
        total = total + part.astype(F32)
    return total


def first_kernel(loads, out):
    lower, root = loads[2].astype(BF16), loads[0].astype(BF16).T
    for chip in range(out.shape[0]):
        side = (chip & 1) * 64
        out[chip, :128, :] = lower
        out[chip, 128:192, :] = root[side : side + 64]


def gather_columns(transposed, own, other, columns):
    first = core_of() == 0
    for chip in range(own.shape[0]):
        mine, theirs = own[chip], other[chip]
        for core in range(2):
            block = jnp.where(first == (core == 0), mine, theirs)
            row = (2 * chip + core) * 128
            columns[row : row + 128, :] = block.T if transposed else block


def partial_of(tile, columns, group):
    rows = tile[group * 128 : group * 128 + 128, :]
    return jnp.dot(rows, columns[...], preferred_element_type=F32).astype(BF16).T


def multiply_kernel(own, other, tile, out, columns):
    gather_columns(True, own, other, columns)
    for group in range(out.shape[0]):
        out[group] = partial_of(tile, columns, group)


def multiply_lower_kernel(own, other, tile, out, columns):
    gather_columns(False, own, other, columns)
    partials = [partial_of(tile, columns, group) for group in range(out.shape[0])]
    first = core_of() == 0
    for group in range(out.shape[0]):
        near = jnp.where(first, partials[group ^ 1], partials[group ^ 3])
        side = (group & 1) * 64
        out[group, :128, :] = partials[group]
        out[group, 128:, :] = near[side : side + 64]


def multiply(kernel, rows, own, other, tile, cost=None):
    return call(
        kernel,
        "multiply",
        array(tile.shape[0] // 128, rows, 128),
        [],
        [own, other, tile],
        [pltpu.VMEM((tile.shape[1], 128), BF16)],
        cost=cost,
    )


def transposed_kernel(gathered, tile, mine, theirs):
    first = core_of() == 0
    rows = jnp.concatenate([gathered[a] for a in range(gathered.shape[0])], axis=1)
    for chip in range(mine.shape[0]):
        column = chip * 256
        product = jnp.dot(rows, tile[:, column : column + 256], preferred_element_type=F32)
        even, odd = product[:, :128], product[:, 128:]
        mine[chip] = jnp.where(first, even, odd)
        theirs[chip] = jnp.where(first, odd, even).astype(BF16)


def multiply_transposed(gathered, tile):
    chips = tile.shape[1] // 256
    return call(
        transposed_kernel,
        "multiply_transposed",
        (array(chips, 128, 128, dtype=F32), array(chips, 128, 128)),
        [],
        [gathered, tile],
    )


def transposed_pair_kernel(gathered, tile, near, mine, theirs):
    first = core_of() == 0
    rows = [
        jnp.concatenate([gathered[a, place] for a in range(gathered.shape[0])], axis=1)
        for place in range(2)
    ]
    for chip in range(mine.shape[0]):
        columns = pl.ds(chip * 256, 256)
        product = jnp.dot(rows[0], tile[:, columns], preferred_element_type=F32)
        product = product + jnp.dot(rows[1], near[:, columns], preferred_element_type=F32)
        even, odd = product[:, :128], product[:, 128:]
        mine[chip] = jnp.where(first, even, odd)
        theirs[chip] = jnp.where(first, odd, even).astype(BF16)


def place_updates(spans, levels, patterns, values, factors, keep, send, sums):
    core = core_of()
    half = keep.shape[0]
    sums[...] = jnp.zeros_like(sums)
    for index, span in enumerate(spans):
        node = node_of(levels[index])

        def chunk(step, carry, index=index, node=node):
            columns = pl.ds(pl.multiple_of(step * 1024, 1024), 1024)
            factor = jnp.concatenate([f[:, columns] for f in factors[index]], axis=0)
            product = jnp.dot(values[index], factor, preferred_element_type=F32)
            for part in range(8):
                block = patterns[index][node, step * 8 + part]
                slot = ((block & 1) ^ core) * half + (block >> 1)
                sums[slot] += product[:, part * 128 : part * 128 + 128]
            return carry

        lax.fori_loop(0, span // 1024, chunk, 0)

    def emit(slot, carry):
        keep[slot] = sums[slot].astype(BF16)
        send[slot] = sums[half + slot].astype(BF16)
        return carry

    lax.fori_loop(0, half, emit, 0, unroll=4)


def lower_kernel(node_blocks, pattern, parts, factor, near, solved, own, far, keep, send, sums):
    leaf, lane = lax.axis_index("leaf"), lax.axis_index("blk")
    total = total_of([parts[g, :128, :] for g in range(parts.shape[0])])
    value = (total * live(node_blocks, 2, lane)).astype(BF16)
    total = total_of([parts[g, 128:, :] for g in range(parts.shape[0])])
    partner = (total * live(node_blocks, 2, lane, leaf_near_of(leaf, lane))).astype(BF16)
    solved[...] = value
    first = side_of() == 0
    low, high = value[:64], value[64:]
    own[...] = jnp.where(first, low, high)
    far[...] = jnp.where(first, high, low)
    values = jnp.concatenate([jnp.where(leaf & 1 == 0, low, high), partner], axis=1)
    spans = (factor.shape[1],)
    place_updates(spans, (2,), [pattern], [values], [[factor, near]], keep, send, sums)


def pair_kernel(node_blocks, pattern, pattern_lower, parts, lower, lower_near, *refs):
    factors, (solved, keep, send, sums) = refs[:4], refs[4:]
    side, lane = side_of(), lax.axis_index("blk")
    for place in range(2):
        which = side if place == 0 else 1 - side
        total = total_of([parts[g, which] for g in range(parts.shape[0])])
        factor = live(node_blocks, 1, near_of(lane) if place else lane)
        solved[place] = (total * factor).astype(BF16)
    values = [
        jnp.concatenate([solved[0], solved[1]], axis=1),
        jnp.concatenate([lower[...], lower_near[...]], axis=1),
    ]
    spans = (factors[0].shape[1], factors[2].shape[1])
    place_updates(
        spans, (1, 2), [pattern, pattern_lower], values, [factors[:2], factors[2:]],
        keep, send, sums,
    )


def rest_kernel(parts, load, copies):
    chip, near = lax.axis_index("blk") >> 1, near_of(lax.axis_index("blk")) >> 1
    for place in range(parts.shape[1]):
        total = total_of([parts[g, place] for g in range(parts.shape[0])])
        given = (chip == place) | (near == place)
        value = (jnp.where(given, load[place].astype(F32), 0.0) - total).astype(BF16)
        for index in range(copies.shape[0]):
            copies[index, place] = value


def rest_middle_kernel(parts, loads, far, copies):
    chip = lax.axis_index("blk") >> 1
    load = loads[1].T
    for place in range(parts.shape[1]):
        total = [total_of([parts[g, place] for g in range(y, parts.shape[0], 2)]) for y in range(2)]
        total = jnp.concatenate(total, axis=0)
        value = (jnp.where(chip == place, load, 0.0) - total).astype(BF16)
        for index in range(copies.shape[0]):
            copies[index, place * 128 : place * 128 + 128, :] = value
    for index in range(copies.shape[0]):
        copies[index, parts.shape[1] * 128 :, :] = far[...]


def join_middle_kernel(parts, out, near):
    for place in range(out.shape[0]):
        rows = pl.ds(place * 128, 128)
        out[place] = total_of([parts[x, rows, :] for x in range(parts.shape[0])]).astype(BF16)
    near[...] = parts[near_of(lax.axis_index("blk")) >> 1, out.shape[0] * 128 :, :]


def join_kernel(parts, out):
    for place in range(out.shape[0]):
        for side in range(2):
            total = parts[side, place].astype(F32) + parts[2 + side, place].astype(F32)
            out[place, side * 64 : side * 64 + 64, :] = total.astype(BF16)


def split_kernel(mine, theirs, out):
    for place in range(mine.shape[0]):
        value = (mine[place] + theirs[place].astype(F32)).astype(BF16)
        for chip in range(out.shape[0]):
            side = (chip & 1) * 64
            out[chip, place] = value[side : side + 64]


def spread_kernel(level, node_blocks, parts, own, near, copies):
    lane = lax.axis_index("blk")
    for place in range(parts.shape[1]):
        value = total_of([parts[x, place] for x in range(parts.shape[0])])
        if level:
            value = value * live(node_blocks, level, 2 * place + (lane & 1))
        value = value.astype(BF16)

        @pl.when(lane >> 1 == place)
        def _():
            own[...] = value

        @pl.when(near_of(lane) >> 1 == place)
        def _():
            near[...] = value

        for index in range(copies.shape[0]):
            copies[index, place] = value


def spread_pair_kernel(node_blocks, mine, far, own, near, copies):
    lane = lax.axis_index("blk")
    for place in range(mine.shape[0]):
        value = mine[place].astype(F32) + far[place].astype(F32)
        value = (value * live(node_blocks, 1, 2 * place + (lane & 1))).astype(BF16)

        @pl.when(lane >> 1 == place)
        def _():
            own[...] = value

        @pl.when(near_of(lane) >> 1 == place)
        def _():
            near[...] = value

        for index in range(copies.shape[0]):
            copies[index, place] = value


def root_kernel(parts, solved, copies):
    value = total_of([parts[g] for g in range(parts.shape[0])]).astype(BF16)
    solved[...] = value
    for index in range(copies.shape[0]):
        copies[index] = value


def pulled_of(level, pattern, own, other, factor, near, chosen):
    core, row_of = core_of(), node_of(level)

    def pick(position, carry):
        block = pattern[row_of, position]
        mine = (block & 1) == core
        column = pl.multiple_of(position * 128, 128)
        chosen[:, pl.ds(column, 128)] = jnp.where(mine, own[block >> 1], other[block >> 1])
        return carry

    lax.fori_loop(0, pattern.shape[1], pick, 0, unroll=4)
    result = []
    for rows in (factor, near):
        product = lax.dot_general(
            rows[...], chosen[...], (((1,), (1,)), ((), ())), preferred_element_type=F32
        )
        result.append(product.T)
    return result


def pull_kernel(level, pattern, own, other, factor, near, out, chosen):
    out[0], out[1] = pulled_of(level, pattern, own, other, factor, near, chosen)


def reduce_kernel(level, paired, pattern, own, other, factor, near, solved, *refs):
    earlier, (copies, chosen) = refs[:-2], refs[-2:]
    side = side_of()
    pulled = pulled_of(level, pattern, own, other, factor, near, chosen)
    for place in range(2):
        value = pulled[place]
        for e in earlier:
            value = value + e[place]
        value = (solved[place].astype(F32) - value).astype(BF16)
        which = place if paired else jnp.where(side == 0, place, 1 - place)
        for index in range(copies.shape[0]):
            copies[index, which] = value


def pull(level, pattern, own, other, factors):
    return call(
        functools.partial(pull_kernel, level),
        "pull",
        array(2, 64, 128, dtype=F32),
        [pattern],
        [own, other, *factors],
        [pltpu.VMEM((64, factors[0].shape[1]), BF16)], 12,
    )


def reduced(level, paired, pattern, own, other, factors, solved, earlier, count):
    return call(
        functools.partial(reduce_kernel, level, paired),
        "reduced",
        array(count, 2, 64, 128),
        [pattern],
        [own, other, *factors, solved, *earlier],
        [pltpu.VMEM((64, factors[0].shape[1]), BF16)], 12,
    )


def whole(mine, far):
    first = side_of() == 0
    low, high = jnp.where(first, mine, far), jnp.where(first, far, mine)
    return jnp.concatenate([low, high], axis=0).T


def stack_kernel(root, middle, lower, far, out):
    out[0] = root[...].T
    out[1] = whole(middle[0], far[2])
    out[2] = lower[...].T


def last_kernel(node_blocks, parts, root, middle, far, out):
    out[0] = whole(root[...], far[0])
    out[1] = whole(middle[...], far[1])
    total = total_of([parts[x] for x in range(parts.shape[0])])
    out[2] = (total * live(node_blocks, 2, lax.axis_index("blk"))).astype(BF16).T


def shards(
    loads,
    inverse_root,
    inverse_middle,
    inverse_lower,
    couple_middle,
    couple_lower,
    couple_between,
    pattern_middle,
    pattern_lower,
    pattern_between,
    node_blocks,
):
    leaf_count = lax.axis_size("leaf")
    block_count = lax.axis_size("blk")
    chip_count = block_count // 2
    chip_groups = [[2 * x + c for x in range(chip_count)] for c in range(2)]
    even_lanes = [i for i in range(block_count) if i >> 1 & 1 == 0]

    def leaf_groups(level):
        size = leaf_count >> level
        return [[g * size + j for j in range(size)] for g in range(1 << level)]

    def pair_groups(level):
        return [
            [leaf * block_count + i for leaf in group for i in (lane, near_of(lane))]
            for group in leaf_groups(level)
            for lane in even_lanes
        ]

    def swap_core(value):
        return lax.ppermute(value, "blk", [(i, i ^ 1) for i in range(block_count)])

    def swap_near(value):
        return lax.ppermute(value, "blk", [(i, near_of(i)) for i in range(block_count)])

    def swap_leaf_near(value):
        pairs = []
        for i in range(leaf_count * block_count):
            leaf, lane = divmod(i, block_count)
            pairs.append((i, leaf_near_of(leaf, lane) * block_count + lane))
        return lax.ppermute(value, ("leaf", "blk"), pairs)

    kept = {}

    def fence(value):
        tied, held = lax.optimization_barrier((value, dict(kept)))
        kept.update(held)
        return tied

    def exchange(value, axis, groups):
        value = fence(value)
        value = lax.all_to_all(value, axis, 0, 0, tiled=True, axis_index_groups=groups)
        return fence(value)

    def over_chips(value):
        return exchange(value, "blk", chip_groups)

    def over_leaf(value, level):
        return exchange(value, "leaf", leaf_groups(level) if level else None)

    def over_pair(value, level):
        size = leaf_count >> level
        value = exchange(value.reshape(2 * size, 64, 128), ("leaf", "blk"), pair_groups(level))
        return value.reshape(size, 2, 64, 128)

    halves = array(chip_count, chip_count, 64, 128)

    def updates(keep, send, level):
        summed = (keep.astype(F32) + swap_core(send).astype(F32)).astype(BF16)
        size = leaf_count >> level
        return over_leaf(summed.reshape((size, chip_count) + keep.shape[1:]), level)

    def backward(gathered, tile):
        mine, theirs = multiply_transposed(gathered, tile)
        return mine, swap_core(theirs)

    def swap_far(value):
        return lax.ppermute(value, "blk", [(i, i ^ 4) for i in range(block_count)])

    def spread_middle(gathered, near):
        tiles = [tile_middle, near]
        mine, theirs = call(
            transposed_pair_kernel, "multiply_transposed",
            (array(chip_count, 64, 128, dtype=F32), array(chip_count, 64, 128)), [],
            [gathered, *tiles],
        )
        mine = (mine + swap_core(theirs).astype(F32)).astype(BF16)
        size = leaf_count >> 1
        kept["own1"], kept["near1"], copies = call(
            spread_pair_kernel, "spread",
            (array(64, 128), array(64, 128), array(size, chip_count, 64, 128)),
            [node_blocks], [mine, swap_far(mine)],
        )
        blocks = over_leaf(copies, 1).reshape(-1, 64, 128)
        return blocks, swap_core(blocks)

    def spread(partial_sums, level):
        size = leaf_count >> level
        parts = over_chips(call(split_kernel, "split", halves, [], partial_sums))
        own, near, copies = call(
            functools.partial(spread_kernel, level), "spread",
            (array(64, 128), array(64, 128), array(size, chip_count, 64, 128)),
            [node_blocks], [parts],
        )
        kept[f"own{level}"], kept[f"near{level}"] = own, near
        blocks = over_leaf(copies, level).reshape(-1, 64, 128)
        return blocks, swap_core(blocks)

    tile_root, tile_middle, tile_lower = inverse_root[0, 0], inverse_middle[0, 0], inverse_lower[0, 0]
    leaf_near_between = swap_leaf_near(couple_between)
    kept["couples"] = [couple_between, couple_lower, couple_middle]

    loaded = over_chips(call(first_kernel, "first", array(chip_count, 192, 128), [], [loads]))
    cost = pl.CostEstimate(flops=int(7.5e9), bytes_accessed=0, transcendentals=0)
    lower = [couple_lower, swap_near(couple_lower)]
    middle = [couple_middle, swap_near(couple_middle)]
    own = loaded[:, :128]
    kept["load_root"] = loaded[:, 128:]
    parts = over_leaf(multiply(multiply_lower_kernel, 192, own, swap_core(own), tile_lower, cost), 2)
    half = (leaf_count >> 1) * chip_count
    parts, lower[1] = lax.optimization_barrier((parts, lower[1]))
    y_lower, own, far, keep, send = call(
        lower_kernel, "lift_lower",
        (array(128, 128), array(64, 128), array(64, 128), array(half, 64, 128), array(half, 64, 128)),
        [node_blocks, pattern_between], [parts, couple_between, leaf_near_between],
        [pltpu.VMEM((2 * half, 64, 128), F32)],
    )
    kept["y_lower"], kept["y_lower_own"], kept["far"], kept["lower"] = y_lower, own, far, lower[1]
    parts = updates(keep, send, 1)
    kept["middle"] = middle[1]
    rows = chip_count * 128 + 64
    parts = over_chips(
        call(
            rest_middle_kernel, "rest", array(chip_count, rows, 128), [],
            [parts, loads, kept.pop("far")],
        )
    )
    own, kept["y_lower_near"] = call(
        join_middle_kernel, "join", (array(chip_count, 128, 128), array(64, 128)), [], [parts]
    )
    parts = over_pair(multiply(multiply_kernel, 128, own, swap_core(own), tile_middle), 1)
    lower[1], middle[1] = kept.pop("lower"), kept.pop("middle")
    near_between = swap_near(kept.pop("couples")[0])
    half = leaf_count * chip_count
    kept["y_middle"], keep, send = call(
        pair_kernel, "lift_pair",
        (array(2, 64, 128), array(half, 64, 128), array(half, 64, 128)),
        [node_blocks, pattern_middle, pattern_lower],
        [parts, kept["y_lower_own"], kept["y_lower_near"], *middle, *lower],
        [pltpu.VMEM((2 * half, 64, 128), F32)], 16,
    )
    parts = updates(keep, send, 0)
    kept["near_between"] = near_between
    kept["tile"] = tile_middle
    parts = over_chips(call(rest_kernel, "rest", halves, [], [parts, kept.pop("load_root")]))
    own = call(join_kernel, "join", array(chip_count, 128, 128), [], [parts])
    near_tile = swap_near(kept.pop("tile"))
    parts = over_leaf(multiply(multiply_kernel, 128, own, swap_core(own), tile_root), 0)
    kept["y_root"], copies = call(
        root_kernel, "root", (array(128, 128), array(leaf_count, 128, 128)), [], [parts]
    )
    partial_sums = backward(over_leaf(copies, 0), tile_root)
    kept["near_tile"] = near_tile
    own, other = spread(partial_sums, 0)
    copies = reduced(
        1, True, pattern_middle, own, other, middle, kept["y_middle"], [], leaf_count >> 1
    )
    kept["own_root"], kept["other_root"] = own, other
    own, other = spread_middle(over_leaf(copies, 1), kept.pop("near_tile"))
    pulled = pull(2, pattern_lower, kept.pop("own_root"), kept.pop("other_root"), lower)
    between = [couple_between, kept.pop("near_between")]
    solved = jnp.stack([kept.pop("y_lower_own"), kept.pop("y_lower_near")])
    copies = reduced(2, False, pattern_between, own, other, between, solved, [pulled], leaf_count >> 2)
    kept["far"] = swap_near(
        jnp.stack([kept.pop("near0"), kept.pop("near1"), kept["y_middle"][1]])
    )
    gathered = over_pair(copies, 2).reshape(-1, 128, 128)
    mine, theirs = backward(gathered, tile_lower)
    kept["forward"] = call(
        stack_kernel, "stack", array(3, 128, 128), [],
        [kept.pop("y_root"), kept.pop("y_middle"), kept.pop("y_lower"), kept["far"]],
    )
    parts = over_chips((mine + theirs.astype(F32)).astype(BF16))
    answer = call(
        last_kernel, "last", array(3, 128, 128), [node_blocks],
        [parts, kept["own0"], kept["own1"], kept["far"]],
    )
    return (kept["forward"], answer)


def solution(mesh):
    in_specs = (
        P(None, ("leaf", "blk"), None),
        P("leaf", "blk", None, None),
        P("leaf", "blk", None, None),
        P("leaf", "blk", None, None),
        P(("leaf", "blk"), None),
        P(("leaf", "blk"), None),
        P(("leaf", "blk"), None),
        P(),
        P(),
        P(),
        P(),
    )
    out_specs = (P(None, ("leaf", "blk"), None), P(None, ("leaf", "blk"), None))
    return jax.shard_map(shards, mesh=mesh, in_specs=in_specs, out_specs=out_specs, check_vma=False)
```

```python
import functools

import jax
import jax.numpy as jnp
from jax import lax
from jax.experimental import pallas as pl
from jax.experimental.pallas import tpu as pltpu
from jax.sharding import PartitionSpec as P

BF16 = jnp.bfloat16
F32 = jnp.float32
MIB = 1024 * 1024
SMEM = pl.BlockSpec(memory_space=pltpu.SMEM)
VMEM = pl.BlockSpec(memory_space=pltpu.VMEM)
ANY = pl.BlockSpec(memory_space=pl.ANY)


def near_of(lane):
    return lane ^ (2 + 4 * (lane & 1))


def core_of():
    return lax.axis_index("blk") & 1


def side_of():
    return lax.axis_index("blk") >> 1 & 1


def node_of(level):
    return lax.axis_index("leaf") // (lax.axis_size("leaf") >> level)


def leaf_near_of(leaf, lane):
    return leaf ^ (1 + 2 * (lane & 1))


def live(node_blocks, level, lane, leaf=None):
    leaf = lax.axis_index("leaf") if leaf is None else leaf
    leaf = leaf % (lax.axis_size("leaf") >> level)
    position = leaf * lax.axis_size("blk") + lane
    limit = node_blocks[2**level - 1 + node_of(level)]
    return jnp.where(position < limit, 1.0, 0.0).astype(F32)


def with_scalars(count, kernel):
    return lambda *refs: kernel(refs[:count], *refs[count:])


def call(kernel, name, out_shape, smem, vmem, scratch=(), limit=24, cost=None, smem_spec=SMEM):
    return pl.pallas_call(
        kernel,
        out_shape=out_shape,
        in_specs=[smem_spec] * len(smem) + [VMEM] * len(vmem),
        out_specs=jax.tree.map(lambda _: VMEM, out_shape),
        scratch_shapes=list(scratch),
        compiler_params=pltpu.CompilerParams(vmem_limit_bytes=limit * MIB),
        cost_estimate=cost,
        name=name,
    )(*smem, *vmem)


def array(*shape, dtype=BF16):
    return jax.ShapeDtypeStruct(shape, dtype)


def total_of(parts):
    total = parts[0].astype(F32)
    for part in parts[1:]:
        total = total + part.astype(F32)
    return total


def first_kernel(loads, out):
    lower, root = loads[2].astype(BF16), loads[0].astype(BF16).T
    for chip in range(out.shape[0]):
        side = (chip & 1) * 64
        out[chip, :128, :] = lower
        out[chip, 128:192, :] = root[side : side + 64]


def gather_columns(transposed, own, other, columns):
    first = core_of() == 0
    for chip in range(own.shape[0]):
        mine, theirs = own[chip], other[chip]
        for core in range(2):
            block = jnp.where(first == (core == 0), mine, theirs)
            row = (2 * chip + core) * 128
            columns[row : row + 128, :] = block.T if transposed else block


def partial_of(tile, columns, group):
    rows = tile[group * 128 : group * 128 + 128, :]
    return jnp.dot(rows, columns[...], preferred_element_type=F32).astype(BF16).T


def multiply_kernel(own, other, tile, out, columns):
    gather_columns(True, own, other, columns)
    for group in range(out.shape[0]):
        out[group] = partial_of(tile, columns, group)


def columns_of(blocks, core, tile, group):
    rows = slice(group * 128, group * 128 + 128)
    factors = [
        tile[rows, pl.ds(pl.multiple_of((2 * chip + core) * 128, 128), 128)]
        for chip in range(blocks.shape[0] // 128)
    ]
    factors = jnp.concatenate(factors, axis=1)
    return jnp.dot(factors, blocks[...], preferred_element_type=F32)


def stack_columns(blocks, columns):
    for chip in range(blocks.shape[0]):
        columns[chip * 128 : chip * 128 + 128, :] = blocks[chip].T


def multiply_own_kernel(own, tile, out, columns):
    stack_columns(own, columns)
    for group in range(out.shape[0]):
        out[group] = columns_of(columns, core_of(), tile, group)


def multiply_rest_kernel(other, mine, tile, out, columns):
    stack_columns(other, columns)
    for group in range(out.shape[0]):
        product = mine[group] + columns_of(columns, 1 - core_of(), tile, group)
        out[group] = product.astype(BF16).T


def multiply_lower_kernel(own, other, tile, out, columns):
    gather_columns(False, own, other, columns)
    partials = [partial_of(tile, columns, group) for group in range(out.shape[0])]
    first = core_of() == 0
    for group in range(out.shape[0]):
        near = jnp.where(first, partials[group ^ 1], partials[group ^ 3])
        side = (group & 1) * 64
        out[group, :128, :] = partials[group]
        out[group, 128:, :] = near[side : side + 64]


def multiply(kernel, rows, own, other, tile, cost=None):
    return call(
        kernel,
        "multiply",
        array(tile.shape[0] // 128, rows, 128),
        [],
        [own, other, tile],
        [pltpu.VMEM((tile.shape[1], 128), BF16)],
        cost=cost,
    )


def transposed_kernel(gathered, tile, mine, theirs):
    first = core_of() == 0
    rows = jnp.concatenate([gathered[a] for a in range(gathered.shape[0])], axis=1)
    for chip in range(mine.shape[0]):
        column = chip * 256
        product = jnp.dot(rows, tile[:, column : column + 256], preferred_element_type=F32)
        even, odd = product[:, :128], product[:, 128:]
        mine[chip] = jnp.where(first, even, odd)
        theirs[chip] = jnp.where(first, odd, even).astype(BF16)


def multiply_transposed(gathered, tile):
    chips = tile.shape[1] // 256
    return call(
        transposed_kernel,
        "multiply_transposed",
        (array(chips, 128, 128, dtype=F32), array(chips, 128, 128)),
        [],
        [gathered, tile],
    )


def transposed_pair_kernel(gathered, tile, near, mine, theirs):
    first = core_of() == 0
    rows = [
        jnp.concatenate([gathered[a, place] for a in range(gathered.shape[0])], axis=1)
        for place in range(2)
    ]
    for chip in range(mine.shape[0]):
        columns = pl.ds(chip * 256, 256)
        product = jnp.dot(rows[0], tile[:, columns], preferred_element_type=F32)
        product = product + jnp.dot(rows[1], near[:, columns], preferred_element_type=F32)
        even, odd = product[:, :128], product[:, 128:]
        mine[chip] = jnp.where(first, even, odd)
        theirs[chip] = jnp.where(first, odd, even).astype(BF16)


def fetch_scalars(sources, targets, semaphores, sums):
    copies = [
        pltpu.make_async_copy(source, target, semaphores.at[index])
        for index, (source, target) in enumerate(zip(sources, targets))
    ]
    for copy in copies:
        copy.start()
    sums[...] = jnp.zeros_like(sums)
    for copy in copies:
        copy.wait()


def scalar_scratch(*sources):
    shapes = [pltpu.SMEM(source.shape, jnp.int32) for source in sources]
    return [*shapes, pltpu.SemaphoreType.DMA((len(sources),))]


def place_updates(spans, levels, patterns, values, factors, keep, send, sums):
    core = core_of()
    half = keep.shape[0]
    for index, span in enumerate(spans):
        node = node_of(levels[index])

        def chunk(step, carry, index=index, node=node):
            columns = pl.ds(pl.multiple_of(step * 1024, 1024), 1024)
            factor = jnp.concatenate([f[:, columns] for f in factors[index]], axis=0)
            product = jnp.dot(values[index], factor, preferred_element_type=F32)
            for part in range(8):
                block = patterns[index][node, step * 8 + part]
                slot = ((block & 1) ^ core) * half + (block >> 1)
                sums[slot] += product[:, part * 128 : part * 128 + 128]
            return carry

        lax.fori_loop(0, span // 1024, chunk, 0, unroll=2)

    def emit(slot, carry):
        keep[slot] = sums[slot].astype(BF16)
        send[slot] = sums[half + slot].astype(BF16)
        return carry

    lax.fori_loop(0, half, emit, 0, unroll=4)


def lower_kernel(
    scalars, parts, factor, near, solved, own, far, masks, keep, send, sums, *scratch
):
    node_blocks, pattern, semaphores = scratch
    fetch_scalars(scalars, scratch[:-1], semaphores, sums)
    leaf, lane = lax.axis_index("leaf"), lax.axis_index("blk")
    total = total_of([parts[g, :128, :] for g in range(parts.shape[0])])
    value = (total * live(node_blocks, 2, lane)).astype(BF16)
    total = total_of([parts[g, 128:, :] for g in range(parts.shape[0])])
    partner = (total * live(node_blocks, 2, lane, leaf_near_of(leaf, lane))).astype(BF16)
    solved[...] = value
    for place in range(masks.shape[0] - 1):
        masks[place] = jnp.full((8, 128), live(node_blocks, 1, 2 * place + (lane & 1)), F32)
    masks[masks.shape[0] - 1] = jnp.full((8, 128), live(node_blocks, 2, lane), F32)
    first = side_of() == 0
    low, high = value[:64], value[64:]
    own[...] = jnp.where(first, low, high)
    far[...] = jnp.where(first, high, low)
    values = jnp.concatenate([jnp.where(leaf & 1 == 0, low, high), partner], axis=1)
    spans = (factor.shape[1],)
    place_updates(spans, (2,), [pattern], [values], [[factor, near]], keep, send, sums)


def pair_kernel(scalars, parts, lower, lower_near, *refs):
    factors, (solved, keep, send, sums, *scratch) = refs[:4], refs[4:]
    node_blocks, pattern, pattern_lower, semaphores = scratch
    fetch_scalars(scalars, scratch[:-1], semaphores, sums)
    side, lane = side_of(), lax.axis_index("blk")
    for place in range(2):
        which = side if place == 0 else 1 - side
        total = total_of([parts[g, which] for g in range(parts.shape[0])])
        factor = live(node_blocks, 1, near_of(lane) if place else lane)
        solved[place] = (total * factor).astype(BF16)
    values = [
        jnp.concatenate([solved[0], solved[1]], axis=1),
        jnp.concatenate([lower[...], lower_near[...]], axis=1),
    ]
    spans = (factors[0].shape[1], factors[2].shape[1])
    place_updates(
        spans, (1, 2), [pattern, pattern_lower], values, [factors[:2], factors[2:]],
        keep, send, sums,
    )


def rest_kernel(parts, load, copies):
    chip, near = lax.axis_index("blk") >> 1, near_of(lax.axis_index("blk")) >> 1
    for place in range(parts.shape[1]):
        total = total_of([parts[g, place] for g in range(parts.shape[0])])
        given = (chip == place) | (near == place)
        value = (jnp.where(given, load[place].astype(F32), 0.0) - total).astype(BF16)
        for index in range(copies.shape[0]):
            copies[index, place] = value


def rest_middle_kernel(parts, loads, far, out):
    chip = lax.axis_index("blk") >> 1
    load = loads[1].T
    for place in range(parts.shape[1]):
        total = [total_of([parts[g, place] for g in range(y, parts.shape[0], 2)]) for y in range(2)]
        total = jnp.concatenate(total, axis=0)
        value = (jnp.where(chip == place, load, 0.0) - total).astype(BF16)
        out[place * 128 : place * 128 + 128, :] = value
    out[parts.shape[1] * 128 :, :] = far[...]


def join_kernel(parts, out):
    for place in range(out.shape[0]):
        for side in range(2):
            total = parts[side, place].astype(F32) + parts[2 + side, place].astype(F32)
            out[place, side * 64 : side * 64 + 64, :] = total.astype(BF16)


def split_kernel(mine, theirs, out):
    for place in range(mine.shape[0]):
        value = (mine[place] + theirs[place].astype(F32)).astype(BF16)
        for chip in range(out.shape[0]):
            side = (chip & 1) * 64
            out[chip, place] = value[side : side + 64]


def spread_kernel(parts, own, near, copies):
    lane = lax.axis_index("blk")
    for place in range(parts.shape[1]):
        value = total_of([parts[x, place] for x in range(parts.shape[0])])
        value = value.astype(BF16)

        @pl.when(lane >> 1 == place)
        def _():
            own[...] = value

        @pl.when(near_of(lane) >> 1 == place)
        def _():
            near[...] = value

        for index in range(copies.shape[0]):
            copies[index, place] = value


def spread_pair_kernel(mine, far, masks, own, near, copies):
    lane = lax.axis_index("blk")
    for place in range(mine.shape[0]):
        value = mine[place].astype(F32) + far[place].astype(F32)
        value = (value * masks[place, :1, :]).astype(BF16)

        @pl.when(lane >> 1 == place)
        def _():
            own[...] = value

        @pl.when(near_of(lane) >> 1 == place)
        def _():
            near[...] = value

        for index in range(copies.shape[0]):
            copies[index, place] = value


def root_kernel(parts, solved, copies):
    value = total_of([parts[g] for g in range(parts.shape[0])]).astype(BF16)
    solved[...] = value
    for index in range(copies.shape[0]):
        copies[index] = value


def pulled_of(level, pattern, own, other, factor, near, chosen):
    core, row_of = core_of(), node_of(level)

    def pick(position, carry):
        block = pattern[row_of, position]
        mine = (block & 1) == core
        column = pl.multiple_of(position * 128, 128)
        chosen[:, pl.ds(column, 128)] = jnp.where(mine, own[block >> 1], other[block >> 1])
        return carry

    lax.fori_loop(0, pattern.shape[1], pick, 0, unroll=4)
    product = jnp.zeros((256, 64), F32)
    for start in range(0, chosen.shape[1], 1024):
        columns = slice(start, start + 1024)
        rows = jnp.concatenate([factor[:, columns], near[:, columns]], axis=0)
        product = product + lax.dot_general(
            rows, chosen[:, columns], (((1,), (1,)), ((), ())), preferred_element_type=F32
        )
    return product[:128].T, product[128:].T


def pull_kernel(level, pattern, own, other, factor, near, out, chosen):
    out[0], out[1] = pulled_of(level, pattern, own, other, factor, near, chosen)


def reduce_kernel(level, paired, pattern, own, other, factor, near, solved, *refs):
    earlier, (copies, chosen) = refs[:-2], refs[-2:]
    side = side_of()
    pulled = pulled_of(level, pattern, own, other, factor, near, chosen)
    for place in range(2):
        value = pulled[place]
        for e in earlier:
            value = value + e[place]
        value = (solved[place].astype(F32) - value).astype(BF16)
        which = place if paired else jnp.where(side == 0, place, 1 - place)
        for index in range(copies.shape[0]):
            copies[index, which] = value


def pull(level, pattern, own, other, factors):
    return call(
        functools.partial(pull_kernel, level),
        "pull",
        array(2, 64, 128, dtype=F32),
        [pattern],
        [own, other, *factors],
        [pltpu.VMEM((64, factors[0].shape[1]), BF16)], 12,
    )


def reduced(level, paired, pattern, own, other, factors, solved, earlier, count):
    return call(
        functools.partial(reduce_kernel, level, paired),
        "reduced",
        array(count, 2, 64, 128),
        [pattern],
        [own, other, *factors, solved, *earlier],
        [pltpu.VMEM((64, factors[0].shape[1]), BF16)], 12,
    )


def whole(mine, far):
    first = side_of() == 0
    low, high = jnp.where(first, mine, far), jnp.where(first, far, mine)
    return jnp.concatenate([low, high], axis=0).T


def stack_kernel(root, middle, lower, far, out):
    out[0] = root[...].T
    out[1] = whole(middle[0], far[2])
    out[2] = lower[...].T


def last_kernel(masks, parts, root, middle, far, out):
    out[0] = whole(root[...], far[0])
    out[1] = whole(middle[...], far[1])
    total = total_of([parts[x] for x in range(parts.shape[0])])
    out[2] = (total * masks[masks.shape[0] - 1, :1, :]).astype(BF16).T


def shards(
    loads,
    inverse_root,
    inverse_middle,
    inverse_lower,
    couple_middle,
    couple_lower,
    couple_between,
    pattern_middle,
    pattern_lower,
    pattern_between,
    node_blocks,
):
    leaf_count = lax.axis_size("leaf")
    block_count = lax.axis_size("blk")
    chip_count = block_count // 2
    chip_groups = [[2 * x + c for x in range(chip_count)] for c in range(2)]
    even_lanes = [i for i in range(block_count) if i >> 1 & 1 == 0]

    def leaf_groups(level):
        size = leaf_count >> level
        return [[g * size + j for j in range(size)] for g in range(1 << level)]

    def pair_groups(level):
        return [
            [leaf * block_count + i for leaf in group for i in (lane, near_of(lane))]
            for group in leaf_groups(level)
            for lane in even_lanes
        ]

    def swap_core(value):
        return lax.ppermute(value, "blk", [(i, i ^ 1) for i in range(block_count)])

    def swap_near(value):
        return lax.ppermute(value, "blk", [(i, near_of(i)) for i in range(block_count)])

    def swap_far(value):
        return lax.ppermute(value, "blk", [(i, i ^ 4) for i in range(block_count)])

    def swap_leaf_near(value):
        pairs = []
        for i in range(leaf_count * block_count):
            leaf, lane = divmod(i, block_count)
            pairs.append((i, leaf_near_of(leaf, lane) * block_count + lane))
        return lax.ppermute(value, ("leaf", "blk"), pairs)

    kept = {}

    def fence(value):
        tied, held = lax.optimization_barrier((value, dict(kept)))
        kept.update(held)
        return tied

    def exchange(value, axis, groups):
        value = fence(value)
        value = lax.all_to_all(value, axis, 0, 0, tiled=True, axis_index_groups=groups)
        return fence(value)

    def over_chips(value):
        return exchange(value, "blk", chip_groups)

    def over_leaf(value, level):
        return exchange(value, "leaf", leaf_groups(level) if level else None)

    def over_pair(value, level):
        size = leaf_count >> level
        value = exchange(value.reshape(2 * size, 64, 128), ("leaf", "blk"), pair_groups(level))
        return value.reshape(size, 2, 64, 128)

    halves = array(chip_count, chip_count, 64, 128)

    def updates(keep, send, level):
        summed = (keep.astype(F32) + swap_core(send).astype(F32)).astype(BF16)
        size = leaf_count >> level
        return over_leaf(summed.reshape((size, chip_count) + keep.shape[1:]), level)

    def backward(gathered, tile):
        mine, theirs = multiply_transposed(gathered, tile)
        return mine, swap_core(theirs)

    def spread_middle(gathered, near):
        tiles = [tile_middle, near]
        mine, theirs = call(
            transposed_pair_kernel, "multiply_transposed",
            (array(chip_count, 64, 128, dtype=F32), array(chip_count, 64, 128)), [],
            [gathered, *tiles],
        )
        mine = (mine + swap_core(theirs).astype(F32)).astype(BF16)
        size = leaf_count >> 1
        kept["pulled"] = pull(
            2, pattern_lower, kept.pop("own_root"), kept.pop("other_root"), kept.pop("lower")
        )
        kept["own1"], kept["near1"], copies = call(
            spread_pair_kernel, "spread",
            (array(64, 128), array(64, 128), array(size, chip_count, 64, 128)),
            [], [mine, swap_far(mine), kept["masks"]],
        )
        blocks = over_leaf(copies, 1).reshape(-1, 64, 128)
        return blocks, swap_core(blocks)

    def spread_root(partial_sums):
        parts = over_chips(call(split_kernel, "split", halves, [], partial_sums))
        kept["own0"], kept["near0"], copies = call(
            spread_kernel, "spread",
            (array(64, 128), array(64, 128), array(leaf_count, chip_count, 64, 128)),
            [], [parts],
        )
        blocks = over_leaf(copies, 0).reshape(-1, 64, 128)
        return blocks, swap_core(blocks)

    tile_root, tile_middle, tile_lower = inverse_root[0, 0], inverse_middle[0, 0], inverse_lower[0, 0]
    leaf_near_between = swap_leaf_near(couple_between)
    kept["couples"] = [couple_between, couple_lower, couple_middle]

    loaded = over_chips(call(first_kernel, "first", array(chip_count, 192, 128), [], [loads]))
    cost = pl.CostEstimate(flops=int(7.5e9), bytes_accessed=0, transcendentals=0)
    lower = [couple_lower, swap_near(couple_lower)]
    middle = [couple_middle, swap_near(couple_middle)]
    own = loaded[:, :128]
    kept["load_root"] = loaded[:, 128:]
    parts = over_leaf(multiply(multiply_lower_kernel, 192, own, swap_core(own), tile_lower, cost), 2)
    half = (leaf_count >> 1) * chip_count
    parts, lower[1] = lax.optimization_barrier((parts, lower[1]))
    y_lower, own, far, kept["masks"], keep, send = call(
        with_scalars(2, lower_kernel), "lift_lower",
        (
            array(128, 128), array(64, 128), array(64, 128),
            array(chip_count + 1, 8, 128, dtype=F32), array(half, 64, 128), array(half, 64, 128),
        ),
        [node_blocks, pattern_between], [parts, couple_between, leaf_near_between],
        [pltpu.VMEM((2 * half, 64, 128), F32), *scalar_scratch(node_blocks, pattern_between)],
        smem_spec=ANY,
    )
    kept["y_lower"], kept["y_lower_own"], kept["far"], kept["lower"] = y_lower, own, far, lower[1]
    parts = updates(keep, send, 1)
    rows = chip_count * 128
    share = call(
        rest_middle_kernel, "rest", array(rows + 64, 128), [], [parts, loads, kept.pop("far")]
    )
    share, middle[1] = lax.optimization_barrier((share, middle[1]))
    near = swap_near(share)
    kept["y_lower_near"] = near[rows:]
    summed = (share[:rows].astype(F32) + near[:rows].astype(F32)).astype(BF16)
    own = (summed.astype(F32) + swap_far(summed).astype(F32)).astype(BF16)
    own = own.reshape(chip_count, 128, 128)
    kept["middle"] = middle[1]
    parts = over_pair(multiply(multiply_kernel, 128, own, swap_core(own), tile_middle), 1)
    lower[1], middle[1] = kept.pop("lower"), kept.pop("middle")
    near_between = swap_near(kept.pop("couples")[0])
    half = leaf_count * chip_count
    kept["y_middle"], keep, send = call(
        with_scalars(3, pair_kernel), "lift_pair",
        (array(2, 64, 128), array(half, 64, 128), array(half, 64, 128)),
        [node_blocks, pattern_middle, pattern_lower],
        [parts, kept["y_lower_own"], kept["y_lower_near"], *middle, *lower],
        [
            pltpu.VMEM((2 * half, 64, 128), F32),
            *scalar_scratch(node_blocks, pattern_middle, pattern_lower),
        ],
        16, smem_spec=ANY,
    )
    parts = updates(keep, send, 0)
    kept["near_between"] = near_between
    kept["tile"] = tile_middle
    parts = over_chips(call(rest_kernel, "rest", halves, [], [parts, kept.pop("load_root")]))
    own = call(join_kernel, "join", array(chip_count, 128, 128), [], [parts])
    near_tile = swap_near(kept.pop("tile"))
    scratch = [pltpu.VMEM((chip_count * 128, 128), BF16)]
    other = swap_core(own)
    mine = call(
        multiply_own_kernel, "multiply_own", array(leaf_count, 128, 128, dtype=F32), [],
        [own, tile_root], scratch,
    )
    parts = call(
        multiply_rest_kernel, "multiply_rest", array(leaf_count, 128, 128), [],
        [other, mine, tile_root], scratch,
    )
    parts = over_leaf(parts, 0)
    kept["y_root"], copies = call(
        root_kernel, "root", (array(128, 128), array(leaf_count, 128, 128)), [], [parts]
    )
    partial_sums = backward(over_leaf(copies, 0), tile_root)
    kept["near_tile"] = near_tile
    own, other = spread_root(partial_sums)
    copies = reduced(
        1, True, pattern_middle, own, other, middle, kept["y_middle"], [], leaf_count >> 1
    )
    kept["own_root"], kept["other_root"], kept["lower"] = own, other, lower
    own, other = spread_middle(over_leaf(copies, 1), kept.pop("near_tile"))
    between = [couple_between, kept.pop("near_between")]
    solved = jnp.stack([kept.pop("y_lower_own"), kept.pop("y_lower_near")])
    copies = reduced(2, False, pattern_between, own, other, between, solved, [kept.pop("pulled")], leaf_count >> 2)
    kept["far"] = swap_near(
        jnp.stack([kept.pop("near0"), kept.pop("near1"), kept["y_middle"][1]])
    )
    gathered = over_pair(copies, 2).reshape(-1, 128, 128)
    mine, theirs = backward(gathered, tile_lower)
    kept["forward"] = call(
        stack_kernel, "stack", array(3, 128, 128), [],
        [kept.pop("y_root"), kept.pop("y_middle"), kept.pop("y_lower"), kept["far"]],
    )
    parts = over_chips((mine + theirs.astype(F32)).astype(BF16))
    answer = call(
        last_kernel, "last", array(3, 128, 128), [],
        [kept["masks"], parts, kept["own0"], kept["own1"], kept["far"]],
    )
    return (kept["forward"], answer)


def solution(mesh):
    in_specs = (
        P(None, ("leaf", "blk"), None),
        P("leaf", "blk", None, None),
        P("leaf", "blk", None, None),
        P("leaf", "blk", None, None),
        P(("leaf", "blk"), None),
        P(("leaf", "blk"), None),
        P(("leaf", "blk"), None),
        P(),
        P(),
        P(),
        P(),
    )
    out_specs = (P(None, ("leaf", "blk"), None), P(None, ("leaf", "blk"), None))
    return jax.shard_map(shards, mesh=mesh, in_specs=in_specs, out_specs=out_specs, check_vma=False)
```

```python
import functools

import jax
import jax.numpy as jnp
from jax import lax
from jax.experimental import pallas as pl
from jax.experimental.pallas import tpu as pltpu
from jax.sharding import PartitionSpec as P

BF16 = jnp.bfloat16
F32 = jnp.float32
MIB = 1024 * 1024
SMEM = pl.BlockSpec(memory_space=pltpu.SMEM)
VMEM = pl.BlockSpec(memory_space=pltpu.VMEM)
ANY = pl.BlockSpec(memory_space=pl.ANY)


def near_of(lane):
    return lane ^ (2 + 4 * (lane & 1))


def core_of():
    return lax.axis_index("blk") & 1


def side_of():
    return lax.axis_index("blk") >> 1 & 1


def node_of(level):
    return lax.axis_index("leaf") // (lax.axis_size("leaf") >> level)


def leaf_near_of(leaf, lane):
    return leaf ^ (1 + 2 * (lane & 1))


def live(node_blocks, level, lane, leaf=None):
    leaf = lax.axis_index("leaf") if leaf is None else leaf
    leaf = leaf % (lax.axis_size("leaf") >> level)
    position = leaf * lax.axis_size("blk") + lane
    limit = node_blocks[2**level - 1 + node_of(level)]
    return jnp.where(position < limit, 1.0, 0.0).astype(F32)


def with_scalars(count, kernel):
    return lambda *refs: kernel(refs[:count], *refs[count:])


def call(kernel, name, out_shape, smem, vmem, scratch=(), limit=24, cost=None, smem_spec=SMEM):
    return pl.pallas_call(
        kernel,
        out_shape=out_shape,
        in_specs=[smem_spec] * len(smem) + [VMEM] * len(vmem),
        out_specs=jax.tree.map(lambda _: VMEM, out_shape),
        scratch_shapes=list(scratch),
        compiler_params=pltpu.CompilerParams(vmem_limit_bytes=limit * MIB),
        cost_estimate=cost,
        name=name,
    )(*smem, *vmem)


def array(*shape, dtype=BF16):
    return jax.ShapeDtypeStruct(shape, dtype)


def total_of(parts):
    total = parts[0].astype(F32)
    for part in parts[1:]:
        total = total + part.astype(F32)
    return total


def gather_columns(transposed, own, other, columns):
    first = core_of() == 0
    for chip in range(own.shape[0]):
        mine, theirs = own[chip], other[chip]
        for core in range(2):
            block = jnp.where(first == (core == 0), mine, theirs)
            row = (2 * chip + core) * 128
            columns[row : row + 128, :] = block.T if transposed else block


def partial_of(tile, columns, group):
    rows = tile[group * 128 : group * 128 + 128, :]
    return jnp.dot(rows, columns[...], preferred_element_type=F32).astype(BF16).T


def columns_of(blocks, core, tile, group):
    rows = slice(group * 128, group * 128 + 128)
    factors = [
        tile[rows, pl.ds(pl.multiple_of((2 * chip + core) * 128, 128), 128)]
        for chip in range(blocks.shape[0] // 128)
    ]
    factors = jnp.concatenate(factors, axis=1)
    return jnp.dot(factors, blocks[...], preferred_element_type=F32)


def stack_columns(blocks, columns):
    for chip in range(blocks.shape[0]):
        columns[chip * 128 : chip * 128 + 128, :] = blocks[chip].T


def multiply_own_kernel(own, tile, out, columns):
    stack_columns(own, columns)
    for group in range(out.shape[0]):
        out[group] = columns_of(columns, core_of(), tile, group)


def multiply_rest_kernel(other, mine, tile, out, columns):
    stack_columns(other, columns)
    for group in range(out.shape[0]):
        product = mine[group] + columns_of(columns, 1 - core_of(), tile, group)
        out[group] = product.astype(BF16).T


def multiply_lower_kernel(own, other, tile, out, columns):
    gather_columns(False, own, other, columns)
    partials = [partial_of(tile, columns, group) for group in range(out.shape[0])]
    first = core_of() == 0
    for group in range(out.shape[0]):
        near = jnp.where(first, partials[group ^ 1], partials[group ^ 3])
        side = (group & 1) * 64
        out[group, :128, :] = partials[group]
        out[group, 128:, :] = near[side : side + 64]


def multiply(kernel, rows, own, other, tile, cost=None):
    return call(
        kernel,
        "multiply",
        array(tile.shape[0] // 128, rows, 128),
        [],
        [own, other, tile],
        [pltpu.VMEM((tile.shape[1], 128), BF16)],
        cost=cost,
    )


def transposed_kernel(gathered, tile, mine, theirs):
    first = core_of() == 0
    rows = jnp.concatenate([gathered[a] for a in range(gathered.shape[0])], axis=1)
    for chip in range(mine.shape[0]):
        column = chip * 256
        product = jnp.dot(rows, tile[:, column : column + 256], preferred_element_type=F32)
        even, odd = product[:, :128], product[:, 128:]
        mine[chip] = jnp.where(first, even, odd)
        theirs[chip] = jnp.where(first, odd, even).astype(BF16)


def multiply_transposed(gathered, tile):
    chips = tile.shape[1] // 256
    return call(
        transposed_kernel,
        "multiply_transposed",
        (array(chips, 128, 128, dtype=F32), array(chips, 128, 128)),
        [],
        [gathered, tile],
    )


def transposed_pair_kernel(gathered, tile, near, mine, theirs):
    first = core_of() == 0
    rows = [
        jnp.concatenate([gathered[a, place] for a in range(gathered.shape[0])], axis=1)
        for place in range(2)
    ]
    for chip in range(mine.shape[0]):
        columns = pl.ds(chip * 256, 256)
        product = jnp.dot(rows[0], tile[:, columns], preferred_element_type=F32)
        product = product + jnp.dot(rows[1], near[:, columns], preferred_element_type=F32)
        even, odd = product[:, :128], product[:, 128:]
        mine[chip] = jnp.where(first, even, odd)
        theirs[chip] = jnp.where(first, odd, even).astype(BF16)


def fetch_scalars(sources, targets, semaphores, sums):
    copies = [
        pltpu.make_async_copy(source, target, semaphores.at[index])
        for index, (source, target) in enumerate(zip(sources, targets))
    ]
    for copy in copies:
        copy.start()
    sums[...] = jnp.zeros_like(sums)
    for copy in copies:
        copy.wait()


def scalar_scratch(*sources):
    shapes = [pltpu.SMEM(source.shape, jnp.int32) for source in sources]
    return [*shapes, pltpu.SemaphoreType.DMA((len(sources),))]


def place_updates(spans, levels, patterns, values, factors, keep, send, sums):
    core = core_of()
    half = keep.shape[0]
    for index, span in enumerate(spans):
        node = node_of(levels[index])

        def chunk(step, carry, index=index, node=node):
            columns = pl.ds(pl.multiple_of(step * 1024, 1024), 1024)
            factor = jnp.concatenate([f[:, columns] for f in factors[index]], axis=0)
            product = jnp.dot(values[index], factor, preferred_element_type=F32)
            for part in range(8):
                block = patterns[index][node, step * 8 + part]
                slot = ((block & 1) ^ core) * half + (block >> 1)
                sums[slot] += product[:, part * 128 : part * 128 + 128]
            return carry

        lax.fori_loop(0, span // 1024, chunk, 0, unroll=4)

    def emit(slot, carry):
        keep[slot] = sums[slot].astype(BF16)
        send[slot] = sums[half + slot].astype(BF16)
        return carry

    lax.fori_loop(0, half, emit, 0, unroll=8)


def lower_kernel(
    scalars, parts, factor, near, solved, own, far, masks, keep, send, sums, *scratch
):
    node_blocks, pattern, semaphores = scratch
    fetch_scalars(scalars, scratch[:-1], semaphores, sums)
    leaf, lane = lax.axis_index("leaf"), lax.axis_index("blk")
    total = total_of([parts[g, :128, :] for g in range(parts.shape[0])])
    value = (total * live(node_blocks, 2, lane)).astype(BF16)
    total = total_of([parts[g, 128:, :] for g in range(parts.shape[0])])
    partner = (total * live(node_blocks, 2, lane, leaf_near_of(leaf, lane))).astype(BF16)
    solved[...] = value
    for place in range(masks.shape[0] - 1):
        masks[place] = jnp.full((8, 128), live(node_blocks, 1, 2 * place + (lane & 1)), F32)
    masks[masks.shape[0] - 1] = jnp.full((8, 128), live(node_blocks, 2, lane), F32)
    first = side_of() == 0
    low, high = value[:64], value[64:]
    own[...] = jnp.where(first, low, high)
    far[...] = jnp.where(first, high, low)
    values = jnp.concatenate([jnp.where(leaf & 1 == 0, low, high), partner], axis=1)
    spans = (factor.shape[1],)
    place_updates(spans, (2,), [pattern], [values], [[factor, near]], keep, send, sums)


def pair_kernel(scalars, parts, lower, lower_near, *refs):
    factors, (solved, keep, send, sums, *scratch) = refs[:4], refs[4:]
    node_blocks, pattern, pattern_lower, semaphores = scratch
    fetch_scalars(scalars, scratch[:-1], semaphores, sums)
    side, lane = side_of(), lax.axis_index("blk")
    for place in range(2):
        which = side if place == 0 else 1 - side
        total = total_of([parts[g, which] for g in range(parts.shape[0])])
        factor = live(node_blocks, 1, near_of(lane) if place else lane)
        solved[place] = (total * factor).astype(BF16)
    values = [
        jnp.concatenate([solved[0], solved[1]], axis=1),
        jnp.concatenate([lower[...], lower_near[...]], axis=1),
    ]
    spans = (factors[0].shape[1], factors[2].shape[1])
    place_updates(
        spans, (1, 2), [pattern, pattern_lower], values, [factors[:2], factors[2:]],
        keep, send, sums,
    )


def rest_kernel(parts, load, load_near, copies):
    chip, near = lax.axis_index("blk") >> 1, near_of(lax.axis_index("blk")) >> 1
    for place in range(parts.shape[1]):
        total = total_of([parts[g, place] for g in range(parts.shape[0])])
        given = jnp.where(chip == place, load[...], load_near[...]).astype(F32)
        value = jnp.where((chip == place) | (near == place), given, 0.0) - total
        value = value.astype(BF16)
        for index in range(copies.shape[0]):
            copies[index, place] = value


def rest_middle_kernel(parts, loads, far, out, load_own):
    chip = lax.axis_index("blk") >> 1
    load = loads[1].T
    for place in range(parts.shape[1]):
        total = [total_of([parts[g, place] for g in range(y, parts.shape[0], 2)]) for y in range(2)]
        total = jnp.concatenate(total, axis=0)
        value = (jnp.where(chip == place, load, 0.0) - total).astype(BF16)
        out[place * 128 : place * 128 + 128, :] = value
    last, root, first = parts.shape[1] * 128, loads[0].astype(BF16).T, side_of() == 0
    out[last : last + 64, :] = far[...]
    out[last + 64 :, :] = jnp.where(first, root[64:], root[:64])
    load_own[...] = jnp.where(first, root[:64], root[64:])


def join_kernel(parts, out):
    for place in range(out.shape[0]):
        for side in range(2):
            total = parts[side, place].astype(F32) + parts[2 + side, place].astype(F32)
            out[place, side * 64 : side * 64 + 64, :] = total.astype(BF16)


def split_kernel(mine, theirs, out):
    for place in range(mine.shape[0]):
        value = (mine[place] + theirs[place].astype(F32)).astype(BF16)
        for chip in range(out.shape[0]):
            side = (chip & 1) * 64
            out[chip, place] = value[side : side + 64]


def spread_kernel(parts, own, near, copies):
    lane = lax.axis_index("blk")
    for place in range(parts.shape[1]):
        value = total_of([parts[x, place] for x in range(parts.shape[0])])
        value = value.astype(BF16)

        @pl.when(lane >> 1 == place)
        def _():
            own[...] = value

        @pl.when(near_of(lane) >> 1 == place)
        def _():
            near[...] = value

        for index in range(copies.shape[0]):
            copies[index, place] = value


def spread_pair_kernel(mine, far, masks, own, near, copies):
    lane = lax.axis_index("blk")
    for place in range(mine.shape[0]):
        value = mine[place].astype(F32) + far[place].astype(F32)
        value = (value * masks[place, :1, :]).astype(BF16)

        @pl.when(lane >> 1 == place)
        def _():
            own[...] = value

        @pl.when(near_of(lane) >> 1 == place)
        def _():
            near[...] = value

        for index in range(copies.shape[0]):
            copies[index, place] = value


def root_kernel(parts, solved, copies):
    value = total_of([parts[g] for g in range(parts.shape[0])]).astype(BF16)
    solved[...] = value
    for index in range(copies.shape[0]):
        copies[index] = value


def pulled_of(level, pattern, own, other, factor, near, chosen):
    core, row_of = core_of(), node_of(level)

    def pick(position, carry):
        block = pattern[row_of, position]
        mine = (block & 1) == core
        column = pl.multiple_of(position * 128, 128)
        chosen[:, pl.ds(column, 128)] = jnp.where(mine, own[block >> 1], other[block >> 1])
        return carry

    lax.fori_loop(0, pattern.shape[1], pick, 0, unroll=16)
    product = jnp.zeros((256, 64), F32)
    for start in range(0, chosen.shape[1], 1024):
        columns = slice(start, start + 1024)
        rows = jnp.concatenate([factor[:, columns], near[:, columns]], axis=0)
        product = product + lax.dot_general(
            rows, chosen[:, columns], (((1,), (1,)), ((), ())), preferred_element_type=F32
        )
    return product[:128].T, product[128:].T


def pull_kernel(level, pattern, own, other, factor, near, out, chosen):
    out[0], out[1] = pulled_of(level, pattern, own, other, factor, near, chosen)


def reduce_kernel(level, paired, pattern, own, other, factor, near, solved, *refs):
    earlier, (copies, chosen) = refs[:-2], refs[-2:]
    side = side_of()
    pulled = pulled_of(level, pattern, own, other, factor, near, chosen)
    for place in range(2):
        value = pulled[place]
        for e in earlier:
            value = value + e[place]
        value = (solved[place].astype(F32) - value).astype(BF16)
        which = place if paired else jnp.where(side == 0, place, 1 - place)
        for index in range(copies.shape[0]):
            copies[index, which] = value


def pull(level, pattern, own, other, factors):
    return call(
        functools.partial(pull_kernel, level),
        "pull",
        array(2, 64, 128, dtype=F32),
        [pattern],
        [own, other, *factors],
        [pltpu.VMEM((64, factors[0].shape[1]), BF16)], 12,
    )


def reduced(level, paired, pattern, own, other, factors, solved, earlier, count):
    return call(
        functools.partial(reduce_kernel, level, paired),
        "reduced",
        array(count, 2, 64, 128),
        [pattern],
        [own, other, *factors, solved, *earlier],
        [pltpu.VMEM((64, factors[0].shape[1]), BF16)], 12,
    )


def whole(mine, far):
    first = side_of() == 0
    low, high = jnp.where(first, mine, far), jnp.where(first, far, mine)
    return jnp.concatenate([low, high], axis=0).T


def stack_kernel(root, middle, lower, far, out):
    out[0] = root[...].T
    out[1] = whole(middle[0], far[2])
    out[2] = lower[...].T


def last_kernel(masks, parts, root, middle, far, out):
    out[0] = whole(root[...], far[0])
    out[1] = whole(middle[...], far[1])
    total = total_of([parts[x] for x in range(parts.shape[0])])
    out[2] = (total * masks[masks.shape[0] - 1, :1, :]).astype(BF16).T


def shards(
    loads,
    inverse_root,
    inverse_middle,
    inverse_lower,
    couple_middle,
    couple_lower,
    couple_between,
    pattern_middle,
    pattern_lower,
    pattern_between,
    node_blocks,
):
    leaf_count = lax.axis_size("leaf")
    block_count = lax.axis_size("blk")
    chip_count = block_count // 2
    chip_groups = [[2 * x + c for x in range(chip_count)] for c in range(2)]
    even_lanes = [i for i in range(block_count) if i >> 1 & 1 == 0]

    def leaf_groups(level):
        size = leaf_count >> level
        return [[g * size + j for j in range(size)] for g in range(1 << level)]

    def pair_groups(level):
        return [
            [leaf * block_count + i for leaf in group for i in (lane, near_of(lane))]
            for group in leaf_groups(level)
            for lane in even_lanes
        ]

    def swap_core(value):
        return lax.ppermute(value, "blk", [(i, i ^ 1) for i in range(block_count)])

    def swap_near(value):
        return lax.ppermute(value, "blk", [(i, near_of(i)) for i in range(block_count)])

    def swap_far(value):
        return lax.ppermute(value, "blk", [(i, i ^ 4) for i in range(block_count)])

    def forward_solve(own, tile):
        count, scratch = tile.shape[0] // 128, [pltpu.VMEM((chip_count * 128, 128), BF16)]
        other = swap_core(own)
        mine = call(
            multiply_own_kernel, "multiply_own", array(count, 128, 128, dtype=F32), [],
            [own, tile], scratch,
        )
        return call(
            multiply_rest_kernel, "multiply_rest", array(count, 128, 128), [],
            [other, mine, tile], scratch,
        )

    def swap_leaf_near(value):
        pairs = []
        for i in range(leaf_count * block_count):
            leaf, lane = divmod(i, block_count)
            pairs.append((i, leaf_near_of(leaf, lane) * block_count + lane))
        return lax.ppermute(value, ("leaf", "blk"), pairs)

    kept = {}

    def fence(value):
        tied, held = lax.optimization_barrier((value, dict(kept)))
        kept.update(held)
        return tied

    def exchange(value, axis, groups):
        value = fence(value)
        value = lax.all_to_all(value, axis, 0, 0, tiled=True, axis_index_groups=groups)
        return fence(value)

    def over_chips(value):
        return exchange(value, "blk", chip_groups)

    def over_leaf(value, level):
        return exchange(value, "leaf", leaf_groups(level) if level else None)

    def over_pair(value, level):
        size = leaf_count >> level
        value = exchange(value.reshape(2 * size, 64, 128), ("leaf", "blk"), pair_groups(level))
        return value.reshape(size, 2, 64, 128)

    halves = array(chip_count, chip_count, 64, 128)

    def updates(keep, send, level):
        summed = (keep.astype(F32) + swap_core(send).astype(F32)).astype(BF16)
        size = leaf_count >> level
        return over_leaf(summed.reshape((size, chip_count) + keep.shape[1:]), level)

    def backward(gathered, tile):
        mine, theirs = multiply_transposed(gathered, tile)
        return mine, swap_core(theirs)

    def spread_middle(gathered, near):
        tiles = [tile_middle, near]
        mine, theirs = call(
            transposed_pair_kernel, "multiply_transposed",
            (array(chip_count, 64, 128, dtype=F32), array(chip_count, 64, 128)), [],
            [gathered, *tiles],
        )
        mine = (mine + swap_core(theirs).astype(F32)).astype(BF16)
        size = leaf_count >> 1
        kept["pulled"] = pull(
            2, pattern_lower, kept.pop("own_root"), kept.pop("other_root"), kept.pop("lower")
        )
        kept["own1"], kept["near1"], copies = call(
            spread_pair_kernel, "spread",
            (array(64, 128), array(64, 128), array(size, chip_count, 64, 128)),
            [], [mine, swap_far(mine), kept["masks"]],
        )
        blocks = over_leaf(copies, 1).reshape(-1, 64, 128)
        return blocks, swap_core(blocks)

    def spread_root(partial_sums):
        parts = over_chips(call(split_kernel, "split", halves, [], partial_sums))
        kept["own0"], kept["near0"], copies = call(
            spread_kernel, "spread",
            (array(64, 128), array(64, 128), array(leaf_count, chip_count, 64, 128)),
            [], [parts],
        )
        blocks = over_leaf(copies, 0).reshape(-1, 64, 128)
        return blocks, swap_core(blocks)

    tile_root, tile_middle, tile_lower = inverse_root[0, 0], inverse_middle[0, 0], inverse_lower[0, 0]
    leaf_near_between = swap_leaf_near(couple_between)
    kept["couples"] = [couple_between, couple_lower, couple_middle]

    load_lower = jnp.broadcast_to(loads[2].astype(BF16)[None], (chip_count, 128, 128))
    own = over_chips(load_lower)
    cost = pl.CostEstimate(flops=int(7.5e9), bytes_accessed=0, transcendentals=0)
    lower = [couple_lower, swap_near(couple_lower)]
    middle = [couple_middle, swap_near(couple_middle)]
    parts = over_leaf(multiply(multiply_lower_kernel, 192, own, swap_core(own), tile_lower, cost), 2)
    half = (leaf_count >> 1) * chip_count
    parts, lower[1] = lax.optimization_barrier((parts, lower[1]))
    y_lower, own, far, kept["masks"], keep, send = call(
        with_scalars(2, lower_kernel), "lift_lower",
        (
            array(128, 128), array(64, 128), array(64, 128),
            array(chip_count + 1, 8, 128, dtype=F32), array(half, 64, 128), array(half, 64, 128),
        ),
        [node_blocks, pattern_between], [parts, couple_between, leaf_near_between],
        [pltpu.VMEM((2 * half, 64, 128), F32), *scalar_scratch(node_blocks, pattern_between)],
        smem_spec=ANY,
    )
    kept["y_lower"], kept["y_lower_own"], kept["far"], kept["lower"] = y_lower, own, far, lower[1]
    parts = updates(keep, send, 1)
    rows = chip_count * 128
    share, kept["load_own"] = call(
        rest_middle_kernel, "rest", (array(rows + 128, 128), array(64, 128)), [],
        [parts, loads, kept.pop("far")],
    )
    share, middle[1] = lax.optimization_barrier((share, middle[1]))
    near = swap_near(share)
    kept["y_lower_near"], kept["load_near"] = near[rows : rows + 64], near[rows + 64 :]
    summed = (share[:rows].astype(F32) + near[:rows].astype(F32)).astype(BF16)
    own = (summed.astype(F32) + swap_far(summed).astype(F32)).astype(BF16)
    own = own.reshape(chip_count, 128, 128)
    kept["middle"] = middle[1]
    parts = over_pair(forward_solve(own, tile_middle), 1)
    lower[1], middle[1] = kept.pop("lower"), kept.pop("middle")
    near_between = swap_near(kept.pop("couples")[0])
    half = leaf_count * chip_count
    kept["y_middle"], keep, send = call(
        with_scalars(3, pair_kernel), "lift_pair",
        (array(2, 64, 128), array(half, 64, 128), array(half, 64, 128)),
        [node_blocks, pattern_middle, pattern_lower],
        [parts, kept["y_lower_own"], kept["y_lower_near"], *middle, *lower],
        [
            pltpu.VMEM((2 * half, 64, 128), F32),
            *scalar_scratch(node_blocks, pattern_middle, pattern_lower),
        ],
        16, smem_spec=ANY,
    )
    parts = updates(keep, send, 0)
    kept["near_between"] = near_between
    kept["tile"] = tile_middle
    parts = over_chips(call(rest_kernel, "rest", halves, [], [parts, kept.pop("load_own"), kept.pop("load_near")]))
    own = call(join_kernel, "join", array(chip_count, 128, 128), [], [parts])
    near_tile = swap_near(kept.pop("tile"))
    parts = forward_solve(own, tile_root)
    parts = over_leaf(parts, 0)
    kept["y_root"], copies = call(
        root_kernel, "root", (array(128, 128), array(leaf_count, 128, 128)), [], [parts]
    )
    partial_sums = backward(over_leaf(copies, 0), tile_root)
    kept["near_tile"] = near_tile
    own, other = spread_root(partial_sums)
    copies = reduced(
        1, True, pattern_middle, own, other, middle, kept["y_middle"], [], leaf_count >> 1
    )
    kept["own_root"], kept["other_root"], kept["lower"] = own, other, lower
    own, other = spread_middle(over_leaf(copies, 1), kept.pop("near_tile"))
    between = [couple_between, kept.pop("near_between")]
    solved = jnp.stack([kept.pop("y_lower_own"), kept.pop("y_lower_near")])
    copies = reduced(2, False, pattern_between, own, other, between, solved, [kept.pop("pulled")], leaf_count >> 2)
    kept["far"] = swap_near(
        jnp.stack([kept.pop("near0"), kept.pop("near1"), kept["y_middle"][1]])
    )
    gathered = over_pair(copies, 2).reshape(-1, 128, 128)
    mine, theirs = backward(gathered, tile_lower)
    kept["forward"] = call(
        stack_kernel, "stack", array(3, 128, 128), [],
        [kept.pop("y_root"), kept.pop("y_middle"), kept.pop("y_lower"), kept["far"]],
    )
    parts = over_chips((mine + theirs.astype(F32)).astype(BF16))
    answer = call(
        last_kernel, "last", array(3, 128, 128), [],
        [kept["masks"], parts, kept["own0"], kept["own1"], kept["far"]],
    )
    return (kept["forward"], answer)


def solution(mesh):
    in_specs = (
        P(None, ("leaf", "blk"), None),
        P("leaf", "blk", None, None),
        P("leaf", "blk", None, None),
        P("leaf", "blk", None, None),
        P(("leaf", "blk"), None),
        P(("leaf", "blk"), None),
        P(("leaf", "blk"), None),
        P(),
        P(),
        P(),
        P(),
    )
    out_specs = (P(None, ("leaf", "blk"), None), P(None, ("leaf", "blk"), None))
    return jax.shard_map(shards, mesh=mesh, in_specs=in_specs, out_specs=out_specs, check_vma=False)
```

```python
import functools

import jax
import jax.numpy as jnp
from jax import lax
from jax.experimental import pallas as pl
from jax.experimental.pallas import tpu as pltpu
from jax.sharding import PartitionSpec as P

BF16 = jnp.bfloat16
F32 = jnp.float32
MIB = 1024 * 1024
SMEM = pl.BlockSpec(memory_space=pltpu.SMEM)
VMEM = pl.BlockSpec(memory_space=pltpu.VMEM)
ANY = pl.BlockSpec(memory_space=pl.ANY)


def near_of(lane):
    return lane ^ (2 + 4 * (lane & 1))


def core_of():
    return lax.axis_index("blk") & 1


def side_of():
    return lax.axis_index("blk") >> 1 & 1


def node_of(level):
    return lax.axis_index("leaf") // (lax.axis_size("leaf") >> level)


def leaf_near_of(leaf, lane):
    return leaf ^ (1 + 2 * (lane & 1))


def live(node_blocks, level, lane, leaf=None):
    leaf = lax.axis_index("leaf") if leaf is None else leaf
    leaf = leaf % (lax.axis_size("leaf") >> level)
    position = leaf * lax.axis_size("blk") + lane
    limit = node_blocks[2**level - 1 + node_of(level)]
    return jnp.where(position < limit, 1.0, 0.0).astype(F32)


def with_scalars(count, kernel):
    return lambda *refs: kernel(refs[:count], *refs[count:])


def call(kernel, name, out_shape, smem, vmem, scratch=(), limit=14, cost=None, smem_spec=SMEM):
    return pl.pallas_call(
        kernel,
        out_shape=out_shape,
        in_specs=[smem_spec] * len(smem) + [VMEM] * len(vmem),
        out_specs=jax.tree.map(lambda _: VMEM, out_shape),
        scratch_shapes=list(scratch),
        compiler_params=pltpu.CompilerParams(vmem_limit_bytes=limit * MIB),
        cost_estimate=cost,
        name=name,
    )(*smem, *vmem)


def array(*shape, dtype=BF16):
    return jax.ShapeDtypeStruct(shape, dtype)


def total_of(parts):
    total = parts[0].astype(F32)
    for part in parts[1:]:
        total = total + part.astype(F32)
    return total


def gather_columns(transposed, own, other, columns):
    first = core_of() == 0
    for chip in range(own.shape[0]):
        mine, theirs = own[chip], other[chip]
        for core in range(2):
            block = jnp.where(first == (core == 0), mine, theirs)
            row = (2 * chip + core) * 128
            columns[row : row + 128, :] = block.T if transposed else block


def partial_of(tile, columns, group):
    rows = tile[group * 128 : group * 128 + 128, :]
    return jnp.dot(rows, columns[...], preferred_element_type=F32).astype(BF16).T


def columns_of(blocks, core, tile, group):
    rows = slice(group * 128, group * 128 + 128)
    factors = [
        tile[rows, pl.ds(pl.multiple_of((2 * chip + core) * 128, 128), 128)]
        for chip in range(blocks.shape[0] // 128)
    ]
    factors = jnp.concatenate(factors, axis=1)
    return jnp.dot(factors, blocks[...], preferred_element_type=F32)


def stack_columns(blocks, columns):
    for chip in range(blocks.shape[0]):
        columns[chip * 128 : chip * 128 + 128, :] = blocks[chip].T


def multiply_own_kernel(own, tile, out, columns):
    stack_columns(own, columns)
    for group in range(out.shape[0]):
        out[group] = columns_of(columns, core_of(), tile, group)


def multiply_rest_kernel(other, mine, tile, out, columns):
    stack_columns(other, columns)
    for group in range(out.shape[0]):
        product = mine[group] + columns_of(columns, 1 - core_of(), tile, group)
        out[group] = product.astype(BF16).T


def multiply_lower_kernel(own, other, tile, out, columns):
    gather_columns(False, own, other, columns)
    partials = [partial_of(tile, columns, group) for group in range(out.shape[0])]
    first = core_of() == 0
    for group in range(out.shape[0]):
        near = jnp.where(first, partials[group ^ 1], partials[group ^ 3])
        side = (group & 1) * 64
        out[group, :128, :] = partials[group]
        out[group, 128:, :] = near[side : side + 64]


def multiply(kernel, rows, own, other, tile, cost=None):
    return call(
        kernel,
        "multiply",
        array(tile.shape[0] // 128, rows, 128),
        [],
        [own, other, tile],
        [pltpu.VMEM((tile.shape[1], 128), BF16)],
        cost=cost,
    )


def transposed_kernel(gathered, tile, mine, theirs):
    first = core_of() == 0
    rows = jnp.concatenate([gathered[a] for a in range(gathered.shape[0])], axis=1)
    for chip in range(mine.shape[0]):
        column = chip * 256
        product = jnp.dot(rows, tile[:, column : column + 256], preferred_element_type=F32)
        even, odd = product[:, :128], product[:, 128:]
        mine[chip] = jnp.where(first, even, odd)
        theirs[chip] = jnp.where(first, odd, even).astype(BF16)


def multiply_transposed(gathered, tile):
    chips = tile.shape[1] // 256
    return call(
        transposed_kernel,
        "multiply_transposed",
        (array(chips, 128, 128, dtype=F32), array(chips, 128, 128)),
        [],
        [gathered, tile],
    )


def transposed_pair_kernel(gathered, tile, near, mine, theirs):
    first = core_of() == 0
    rows = [
        jnp.concatenate([gathered[a, place] for a in range(gathered.shape[0])], axis=1)
        for place in range(2)
    ]
    for chip in range(mine.shape[0]):
        columns = pl.ds(chip * 256, 256)
        product = jnp.dot(rows[0], tile[:, columns], preferred_element_type=F32)
        product = product + jnp.dot(rows[1], near[:, columns], preferred_element_type=F32)
        even, odd = product[:, :128], product[:, 128:]
        mine[chip] = jnp.where(first, even, odd)
        theirs[chip] = jnp.where(first, odd, even).astype(BF16)


def fetch_scalars(sources, targets, semaphores, sums):
    copies = [
        pltpu.make_async_copy(source, target, semaphores.at[index])
        for index, (source, target) in enumerate(zip(sources, targets))
    ]
    for copy in copies:
        copy.start()
    sums[...] = jnp.zeros_like(sums)
    for copy in copies:
        copy.wait()


def scalar_scratch(*sources):
    shapes = [pltpu.SMEM(source.shape, jnp.int32) for source in sources]
    return [*shapes, pltpu.SemaphoreType.DMA((len(sources),))]


def place_updates(spans, levels, patterns, values, factors, keep, send, sums):
    core = core_of()
    half = keep.shape[0]
    for index, span in enumerate(spans):
        node = node_of(levels[index])

        def chunk(step, carry, index=index, node=node):
            columns = pl.ds(pl.multiple_of(step * 1024, 1024), 1024)
            factor = jnp.concatenate([f[:, columns] for f in factors[index]], axis=0)
            product = jnp.dot(values[index], factor, preferred_element_type=F32)
            for part in range(8):
                block = patterns[index][node, step * 8 + part]
                slot = ((block & 1) ^ core) * half + (block >> 1)
                sums[slot] += product[:, part * 128 : part * 128 + 128]
            return carry

        lax.fori_loop(0, span // 1024, chunk, 0, unroll=4)

    def emit(slot, carry):
        keep[slot] = sums[slot].astype(BF16)
        send[slot] = sums[half + slot].astype(BF16)
        return carry

    lax.fori_loop(0, half, emit, 0, unroll=8)


def lower_kernel(
    scalars, parts, factor, near, solved, own, far, masks, keep, send, sums, *scratch
):
    node_blocks, pattern, semaphores = scratch
    fetch_scalars(scalars, scratch[:-1], semaphores, sums)
    leaf, lane = lax.axis_index("leaf"), lax.axis_index("blk")
    total = total_of([parts[g, :128, :] for g in range(parts.shape[0])])
    value = (total * live(node_blocks, 2, lane)).astype(BF16)
    total = total_of([parts[g, 128:, :] for g in range(parts.shape[0])])
    partner = (total * live(node_blocks, 2, lane, leaf_near_of(leaf, lane))).astype(BF16)
    solved[...] = value
    for place in range(masks.shape[0] - 1):
        masks[place] = jnp.full((8, 128), live(node_blocks, 1, 2 * place + (lane & 1)), F32)
    masks[masks.shape[0] - 1] = jnp.full((8, 128), live(node_blocks, 2, lane), F32)
    first = side_of() == 0
    low, high = value[:64], value[64:]
    own[...] = jnp.where(first, low, high)
    far[...] = jnp.where(first, high, low)
    values = jnp.concatenate([jnp.where(leaf & 1 == 0, low, high), partner], axis=1)
    spans = (factor.shape[1],)
    place_updates(spans, (2,), [pattern], [values], [[factor, near]], keep, send, sums)


def pair_kernel(scalars, parts, lower, lower_near, *refs):
    factors, (solved, keep, send, sums, *scratch) = refs[:4], refs[4:]
    node_blocks, pattern, pattern_lower, semaphores = scratch
    fetch_scalars(scalars, scratch[:-1], semaphores, sums)
    side, lane = side_of(), lax.axis_index("blk")
    for place in range(2):
        which = side if place == 0 else 1 - side
        total = total_of([parts[g, which] for g in range(parts.shape[0])])
        factor = live(node_blocks, 1, near_of(lane) if place else lane)
        solved[place] = (total * factor).astype(BF16)
    values = [
        jnp.concatenate([solved[0], solved[1]], axis=1),
        jnp.concatenate([lower[...], lower_near[...]], axis=1),
    ]
    spans = (factors[0].shape[1], factors[2].shape[1])
    place_updates(
        spans, (1, 2), [pattern, pattern_lower], values, [factors[:2], factors[2:]],
        keep, send, sums,
    )


def rest_kernel(parts, load, load_near, copies):
    chip, near = lax.axis_index("blk") >> 1, near_of(lax.axis_index("blk")) >> 1
    for place in range(parts.shape[1]):
        total = total_of([parts[g, place] for g in range(parts.shape[0])])
        given = jnp.where(chip == place, load[...], load_near[...]).astype(F32)
        value = jnp.where((chip == place) | (near == place), given, 0.0) - total
        value = value.astype(BF16)
        for index in range(copies.shape[0]):
            copies[index, place] = value


def rest_middle_kernel(parts, loads, far, out, load_own):
    chip = lax.axis_index("blk") >> 1
    load = loads[1].T
    for place in range(parts.shape[1]):
        total = [total_of([parts[g, place] for g in range(y, parts.shape[0], 2)]) for y in range(2)]
        total = jnp.concatenate(total, axis=0)
        value = (jnp.where(chip == place, load, 0.0) - total).astype(BF16)
        out[place * 128 : place * 128 + 128, :] = value
    last, root, first = parts.shape[1] * 128, loads[0].astype(BF16).T, side_of() == 0
    out[last : last + 64, :] = far[...]
    out[last + 64 :, :] = jnp.where(first, root[64:], root[:64])
    load_own[...] = jnp.where(first, root[:64], root[64:])


def join_kernel(parts, out):
    for place in range(out.shape[0]):
        for side in range(2):
            total = parts[side, place].astype(F32) + parts[2 + side, place].astype(F32)
            out[place, side * 64 : side * 64 + 64, :] = total.astype(BF16)


def split_kernel(mine, theirs, out):
    for place in range(mine.shape[0]):
        value = (mine[place] + theirs[place].astype(F32)).astype(BF16)
        for chip in range(out.shape[0]):
            side = (chip & 1) * 64
            out[chip, place] = value[side : side + 64]


def spread_kernel(parts, own, near, copies):
    lane = lax.axis_index("blk")
    for place in range(parts.shape[1]):
        value = total_of([parts[x, place] for x in range(parts.shape[0])])
        value = value.astype(BF16)

        @pl.when(lane >> 1 == place)
        def _():
            own[...] = value

        @pl.when(near_of(lane) >> 1 == place)
        def _():
            near[...] = value

        for index in range(copies.shape[0]):
            copies[index, place] = value


def spread_pair_kernel(mine, far, masks, own, near, copies):
    lane = lax.axis_index("blk")
    for place in range(mine.shape[0]):
        value = mine[place].astype(F32) + far[place].astype(F32)
        value = (value * masks[place, :1, :]).astype(BF16)

        @pl.when(lane >> 1 == place)
        def _():
            own[...] = value

        @pl.when(near_of(lane) >> 1 == place)
        def _():
            near[...] = value

        for index in range(copies.shape[0]):
            copies[index, place] = value


def root_kernel(parts, solved, copies):
    value = total_of([parts[g] for g in range(parts.shape[0])]).astype(BF16)
    solved[...] = value
    for index in range(copies.shape[0]):
        copies[index] = value


def pulled_of(level, pattern, own, other, factor, near, chosen):
    core, row_of = core_of(), node_of(level)

    def pick(position, carry):
        block = pattern[row_of, position]
        mine = (block & 1) == core
        column = pl.multiple_of(position * 128, 128)
        chosen[:, pl.ds(column, 128)] = jnp.where(mine, own[block >> 1], other[block >> 1])
        return carry

    lax.fori_loop(0, pattern.shape[1], pick, 0, unroll=16)
    product = jnp.zeros((256, 64), F32)
    for start in range(0, chosen.shape[1], 1024):
        columns = slice(start, start + 1024)
        rows = jnp.concatenate([factor[:, columns], near[:, columns]], axis=0)
        product = product + lax.dot_general(
            rows, chosen[:, columns], (((1,), (1,)), ((), ())), preferred_element_type=F32
        )
    return product[:128].T, product[128:].T


def pull_kernel(level, pattern, own, other, factor, near, out, chosen):
    out[0], out[1] = pulled_of(level, pattern, own, other, factor, near, chosen)


def reduce_kernel(level, paired, pattern, own, other, factor, near, solved, *refs):
    earlier, (copies, chosen) = refs[:-2], refs[-2:]
    side = side_of()
    pulled = pulled_of(level, pattern, own, other, factor, near, chosen)
    for place in range(2):
        value = pulled[place]
        for e in earlier:
            value = value + e[place]
        value = (solved[place].astype(F32) - value).astype(BF16)
        which = place if paired else jnp.where(side == 0, place, 1 - place)
        for index in range(copies.shape[0]):
            copies[index, which] = value


def pull(level, pattern, own, other, factors):
    return call(
        functools.partial(pull_kernel, level),
        "pull",
        array(2, 64, 128, dtype=F32),
        [pattern],
        [own, other, *factors],
        [pltpu.VMEM((64, factors[0].shape[1]), BF16)], 12,
    )


def reduced(level, paired, pattern, own, other, factors, solved, earlier, count):
    return call(
        functools.partial(reduce_kernel, level, paired),
        "reduced",
        array(count, 2, 64, 128),
        [pattern],
        [own, other, *factors, solved, *earlier],
        [pltpu.VMEM((64, factors[0].shape[1]), BF16)], 12,
    )


def whole(mine, far):
    first = side_of() == 0
    low, high = jnp.where(first, mine, far), jnp.where(first, far, mine)
    return jnp.concatenate([low, high], axis=0).T


def stack_kernel(root, middle, lower, far, out):
    out[0] = root[...].T
    out[1] = whole(middle[0], far[2])
    out[2] = lower[...].T


def last_kernel(masks, parts, root, middle, far, out):
    out[0] = whole(root[...], far[0])
    out[1] = whole(middle[...], far[1])
    total = total_of([parts[x] for x in range(parts.shape[0])])
    out[2] = (total * masks[masks.shape[0] - 1, :1, :]).astype(BF16).T


def shards(
    loads,
    inverse_root,
    inverse_middle,
    inverse_lower,
    couple_middle,
    couple_lower,
    couple_between,
    pattern_middle,
    pattern_lower,
    pattern_between,
    node_blocks,
):
    leaf_count = lax.axis_size("leaf")
    block_count = lax.axis_size("blk")
    chip_count = block_count // 2
    chip_groups = [[2 * x + c for x in range(chip_count)] for c in range(2)]
    even_lanes = [i for i in range(block_count) if i >> 1 & 1 == 0]

    def leaf_groups(level):
        size = leaf_count >> level
        return [[g * size + j for j in range(size)] for g in range(1 << level)]

    def pair_groups(level):
        return [
            [leaf * block_count + i for leaf in group for i in (lane, near_of(lane))]
            for group in leaf_groups(level)
            for lane in even_lanes
        ]

    def swap_core(value):
        return lax.ppermute(value, "blk", [(i, i ^ 1) for i in range(block_count)])

    def swap_near(value):
        return lax.ppermute(value, "blk", [(i, near_of(i)) for i in range(block_count)])

    def swap_far(value):
        return lax.ppermute(value, "blk", [(i, i ^ 4) for i in range(block_count)])

    def forward_solve(own, tile):
        count, scratch = tile.shape[0] // 128, [pltpu.VMEM((chip_count * 128, 128), BF16)]
        other = swap_core(own)
        mine = call(
            multiply_own_kernel, "multiply_own", array(count, 128, 128, dtype=F32), [],
            [own, tile], scratch,
        )
        return call(
            multiply_rest_kernel, "multiply_rest", array(count, 128, 128), [],
            [other, mine, tile], scratch,
        )

    def swap_leaf_near(value):
        pairs = []
        for i in range(leaf_count * block_count):
            leaf, lane = divmod(i, block_count)
            pairs.append((i, leaf_near_of(leaf, lane) * block_count + lane))
        return lax.ppermute(value, ("leaf", "blk"), pairs)

    kept = {}

    def fence(value):
        tied, held = lax.optimization_barrier((value, dict(kept)))
        kept.update(held)
        return tied

    def exchange(value, axis, groups):
        value = fence(value)
        value = lax.all_to_all(value, axis, 0, 0, tiled=True, axis_index_groups=groups)
        return fence(value)

    def over_chips(value):
        return exchange(value, "blk", chip_groups)

    def over_leaf(value, level):
        return exchange(value, "leaf", leaf_groups(level) if level else None)

    def over_pair(value, level):
        size = leaf_count >> level
        value = exchange(value.reshape(2 * size, 64, 128), ("leaf", "blk"), pair_groups(level))
        return value.reshape(size, 2, 64, 128)

    halves = array(chip_count, chip_count, 64, 128)

    def updates(keep, send, level):
        summed = (keep.astype(F32) + swap_core(send).astype(F32)).astype(BF16)
        size = leaf_count >> level
        return over_leaf(summed.reshape((size, chip_count) + keep.shape[1:]), level)

    def backward(gathered, tile):
        mine, theirs = multiply_transposed(gathered, tile)
        return mine, swap_core(theirs)

    def spread_middle(gathered, near):
        tiles = [tile_middle, near]
        mine, theirs = call(
            transposed_pair_kernel, "multiply_transposed",
            (array(chip_count, 64, 128, dtype=F32), array(chip_count, 64, 128)), [],
            [gathered, *tiles],
        )
        mine = (mine + swap_core(theirs).astype(F32)).astype(BF16)
        size = leaf_count >> 1
        kept["pulled"] = pull(
            2, pattern_lower, kept.pop("own_root"), kept.pop("other_root"), kept.pop("lower")
        )
        kept["own1"], kept["near1"], copies = call(
            spread_pair_kernel, "spread",
            (array(64, 128), array(64, 128), array(size, chip_count, 64, 128)),
            [], [mine, swap_far(mine), kept["masks"]],
        )
        blocks = over_leaf(copies, 1).reshape(-1, 64, 128)
        return blocks, swap_core(blocks)

    def spread_root(partial_sums):
        parts = over_chips(call(split_kernel, "split", halves, [], partial_sums))
        kept["own0"], kept["near0"], copies = call(
            spread_kernel, "spread",
            (array(64, 128), array(64, 128), array(leaf_count, chip_count, 64, 128)),
            [], [parts],
        )
        blocks = over_leaf(copies, 0).reshape(-1, 64, 128)
        return blocks, swap_core(blocks)

    tile_root, tile_middle, tile_lower = inverse_root[0, 0], inverse_middle[0, 0], inverse_lower[0, 0]
    leaf_near_between = swap_leaf_near(couple_between)
    kept["couples"] = [couple_between, couple_lower, couple_middle]

    load_lower = jnp.broadcast_to(loads[2].astype(BF16)[None], (chip_count, 128, 128))
    own = over_chips(load_lower)
    cost = pl.CostEstimate(flops=int(7.5e9), bytes_accessed=0, transcendentals=0)
    lower = [couple_lower, swap_near(couple_lower)]
    middle = [couple_middle, swap_near(couple_middle)]
    parts = over_leaf(multiply(multiply_lower_kernel, 192, own, swap_core(own), tile_lower, cost), 2)
    half = (leaf_count >> 1) * chip_count
    parts, lower[1] = lax.optimization_barrier((parts, lower[1]))
    y_lower, own, far, kept["masks"], keep, send = call(
        with_scalars(2, lower_kernel), "lift_lower",
        (
            array(128, 128), array(64, 128), array(64, 128),
            array(chip_count + 1, 8, 128, dtype=F32), array(half, 64, 128), array(half, 64, 128),
        ),
        [node_blocks, pattern_between], [parts, couple_between, leaf_near_between],
        [pltpu.VMEM((2 * half, 64, 128), F32), *scalar_scratch(node_blocks, pattern_between)],
        smem_spec=ANY,
    )
    kept["y_lower"], kept["y_lower_own"], kept["far"], kept["lower"] = y_lower, own, far, lower[1]
    parts = updates(keep, send, 1)
    rows = chip_count * 128
    share, kept["load_own"] = call(
        rest_middle_kernel, "rest", (array(rows + 128, 128), array(64, 128)), [],
        [parts, loads, kept.pop("far")],
    )
    share, middle[1] = lax.optimization_barrier((share, middle[1]))
    near = swap_near(share)
    kept["y_lower_near"], kept["load_near"] = near[rows : rows + 64], near[rows + 64 :]
    summed = (share[:rows].astype(F32) + near[:rows].astype(F32)).astype(BF16)
    own = (summed.astype(F32) + swap_far(summed).astype(F32)).astype(BF16)
    own = own.reshape(chip_count, 128, 128)
    kept["middle"] = middle[1]
    parts = over_pair(forward_solve(own, tile_middle), 1)
    lower[1], middle[1] = kept.pop("lower"), kept.pop("middle")
    near_between = swap_near(kept.pop("couples")[0])
    half = leaf_count * chip_count
    kept["y_middle"], keep, send = call(
        with_scalars(3, pair_kernel), "lift_pair",
        (array(2, 64, 128), array(half, 64, 128), array(half, 64, 128)),
        [node_blocks, pattern_middle, pattern_lower],
        [parts, kept["y_lower_own"], kept["y_lower_near"], *middle, *lower],
        [
            pltpu.VMEM((2 * half, 64, 128), F32),
            *scalar_scratch(node_blocks, pattern_middle, pattern_lower),
        ],
        16, smem_spec=ANY,
    )
    parts = updates(keep, send, 0)
    kept["near_between"] = near_between
    kept["tile"] = tile_middle
    parts = over_chips(call(rest_kernel, "rest", halves, [], [parts, kept.pop("load_own"), kept.pop("load_near")]))
    own = call(join_kernel, "join", array(chip_count, 128, 128), [], [parts])
    near_tile = swap_near(kept.pop("tile"))
    parts = forward_solve(own, tile_root)
    parts = over_leaf(parts, 0)
    kept["y_root"], copies = call(
        root_kernel, "root", (array(128, 128), array(leaf_count, 128, 128)), [], [parts]
    )
    partial_sums = backward(over_leaf(copies, 0), tile_root)
    kept["near_tile"] = near_tile
    own, other = spread_root(partial_sums)
    copies = reduced(
        1, True, pattern_middle, own, other, middle, kept["y_middle"], [], leaf_count >> 1
    )
    kept["own_root"], kept["other_root"], kept["lower"] = own, other, lower
    own, other = spread_middle(over_leaf(copies, 1), kept.pop("near_tile"))
    between = [couple_between, kept.pop("near_between")]
    solved = jnp.stack([kept.pop("y_lower_own"), kept.pop("y_lower_near")])
    copies = reduced(2, False, pattern_between, own, other, between, solved, [kept.pop("pulled")], leaf_count >> 2)
    kept["far"] = swap_near(
        jnp.stack([kept.pop("near0"), kept.pop("near1"), kept["y_middle"][1]])
    )
    gathered = over_pair(copies, 2).reshape(-1, 128, 128)
    mine, theirs = backward(gathered, tile_lower)
    kept["forward"] = call(
        stack_kernel, "stack", array(3, 128, 128), [],
        [kept.pop("y_root"), kept.pop("y_middle"), kept.pop("y_lower"), kept["far"]],
    )
    parts = over_chips((mine + theirs.astype(F32)).astype(BF16))
    answer = call(
        last_kernel, "last", array(3, 128, 128), [],
        [kept["masks"], parts, kept["own0"], kept["own1"], kept["far"]],
    )
    return (kept["forward"], answer)


def solution(mesh):
    in_specs = (
        P(None, ("leaf", "blk"), None),
        P("leaf", "blk", None, None),
        P("leaf", "blk", None, None),
        P("leaf", "blk", None, None),
        P(("leaf", "blk"), None),
        P(("leaf", "blk"), None),
        P(("leaf", "blk"), None),
        P(),
        P(),
        P(),
        P(),
    )
    out_specs = (P(None, ("leaf", "blk"), None), P(None, ("leaf", "blk"), None))
    return jax.shard_map(shards, mesh=mesh, in_specs=in_specs, out_specs=out_specs, check_vma=False)
```
